32 devices in a mesh: seq: 4 (over z), row: 2 (over x), col: 4 (over y, core).
Axes of the slice: x: 2, y: 2, z: 4, core: 2. Of those that a mesh axis runs over, the one named last changes fastest.
Arguments:
- tokens: float32 [1600, 4096], P('row', ('seq', 'col')), may hold values from -6 to 6
- cotangent: float32 [1600, 4096], P('row', ('seq', 'col')), may hold values from -6 to 6
- norm_gain: float32 [2, 2, 1600], P(None, None, 'row'), may hold values from 0.25 to 1.75
- norm_bias: float32 [2, 2, 1600], P(None, None, 'row'), may hold values from -2 to 2
- w_qkv: float32 [2, 1600, 3, 1600], P(None, 'row', None, 'col'), may hold values from -0.15625 to 0.15625
- b_qv: float32 [2, 2, 1600], P(None, None, 'col'), may hold values from -2 to 2
- w_out: float32 [2, 1600, 1600], P(None, 'row', 'col'), may hold values from -0.625 to 0.625
- out_bias: float32 [2, 2, 1600], P(None, None, 'row'), may hold values from -2 to 2
- w_fc: float32 [2, 1600, 6400], P(None, 'row', 'col'), may hold values from -0.15625 to 0.15625
- b_fc: float32 [2, 6400], P(None, 'col'), may hold values from -2 to 2
- w_proj: float32 [2, 1600, 6400], P(None, 'row', 'col'), may hold values from -0.078125 to 0.078125
Outputs:
- stream_out: float32 [1600, 4096], P('row', ('seq', 'col'))
- grad_tokens: float32 [1600, 4096], P('row', ('seq', 'col'))
- grad_norm_gain: float32 [2, 2, 1600], P(None, None, 'row')
- grad_norm_bias: float32 [2, 2, 1600], P(None, None, 'row')
- grad_w_qkv: float32 [2, 1600, 3, 1600], P(None, 'row', None, 'col')
- grad_b_qv: float32 [2, 2, 1600], P(None, None, 'col')
- grad_w_out: float32 [2, 1600, 1600], P(None, 'row', 'col')
- grad_out_bias: float32 [2, 2, 1600], P(None, None, 'row')
- grad_w_fc: float32 [2, 1600, 6400], P(None, 'row', 'col')
- grad_b_fc: float32 [2, 6400], P(None, 'col')
- grad_w_proj: float32 [2, 1600, 6400], P(None, 'row', 'col')
The draws below stay inside these ranges and needn't reach their ends.
All inputs are finite; a program needn't handle non-finite values.
Results may differ from the reference program's by a relative error of at most 0.035.
Values may be sent and summed in bfloat16 or wider, within the bound.
A program may use at most 384 MiB of HBM per device.

```python
import jax
import jax.numpy as jnp
from jax import lax

HEADS = 25
HDIM = 64
D = 1600
FF = 6400
LAYERS = 2
SPAN = 256
SEQS = 4
TOKENS = 4096
N_SEQ = 4


def block_levels(key, extent, split, smallest, top_value):
    loudness = 1.0
    for position, shards_of in split:
        steps = jax.random.uniform(jax.random.fold_in(jax.random.fold_in(key, 6), position), (shards_of,), jnp.float32, smallest / len(split), top_value / len(split))
        loudness = loudness * jnp.repeat(jnp.exp(steps), extent[position] // shards_of).reshape((-1,) + (1,) * (len(extent) - 1 - position))
    return loudness


def bell_draw(rng, dims, width, most, pieces=(), kind=jnp.bfloat16):
    entries = jax.random.normal(rng, dims, jnp.float32) * width
    if len(pieces) > 0:
        entries = block_levels(rng, dims, pieces, -0.22, 0.18) * entries
    return jnp.clip(entries, min=-most, max=most).astype(kind)


def setup_inputs(seed: int = 0) -> dict:
    splits = jax.random.split(jax.random.key(seed), 12)
    return {
        "tokens": bell_draw(splits[0], (D, TOKENS), 1.0, 6.0, ((0, 2), (1, 16)), jnp.float32),
        "cotangent": bell_draw(splits[1], (D, TOKENS), 1.0, 6.0, ((0, 2), (1, 16)), jnp.float32),
        "norm_gain": jnp.clip(1.0 + 0.15 * jax.random.normal(splits[2], (LAYERS, 2, D), jnp.float32), 0.25, 1.75),
        "norm_bias": bell_draw(splits[3], (LAYERS, 2, D), 0.3, 2.0, ((2, 2),), jnp.float32),
        "w_qkv": bell_draw(splits[4], (LAYERS, D, 3, D), D ** -0.5, 0.15625, ((1, 2), (3, 4)), jnp.float32),
        "b_qv": bell_draw(splits[5], (LAYERS, 2, D), 0.3, 2.0, ((2, 4),), jnp.float32),
        "w_out": bell_draw(splits[6], (LAYERS, D, D), (D // 16) ** -0.5, 0.625, ((1, 2), (2, 4)), jnp.float32),
        "out_bias": bell_draw(splits[7], (LAYERS, 2, D), 0.3, 2.0, ((2, 2),), jnp.float32),
        "w_fc": bell_draw(splits[8], (LAYERS, D, FF), D ** -0.5, 0.15625, ((1, 2), (2, 4)), jnp.float32),
        "b_fc": bell_draw(splits[9], (LAYERS, FF), 0.3, 2.0, ((1, 4),), jnp.float32),
        "w_proj": bell_draw(splits[10], (LAYERS, D, FF), FF ** -0.5, 0.078125, ((1, 2), (2, 4)), jnp.float32),
    }


@jax.custom_vjp
def low(v):
    return lax.optimization_barrier(v.astype(jnp.bfloat16)).astype(jnp.float32)

@jax.custom_vjp
def low_back(v):
    return v

def low_keep(v):
    return (low(v), None)

def low_pass(kept, grad):
    return (grad,)

def back_keep(v):
    return (v, None)

def back_low(kept, grad):
    return (low(grad),)
low.defvjp(low_keep, low_pass)
low_back.defvjp(back_keep, back_low)

def dot_exact(left, right):
    return jnp.dot(left, right, precision=lax.Precision.HIGHEST)

def layer_norm(values, gain, shift):
    mean_value = lax.optimization_barrier(jnp.mean(values, axis=-1, keepdims=True))
    centred = values - mean_value
    variance = lax.optimization_barrier(jnp.mean(centred * centred, axis=-1, keepdims=True))
    return centred * lax.rsqrt(variance + 1e-05) * gain + shift

def attend_sequence(inputs):
    query, keys, values = inputs
    raw = low_back(jnp.einsum('qhe,khe->hqk', query, keys, precision=lax.Precision.HIGHEST))
    scores = raw * HDIM ** (-0.5)
    places = jnp.arange(query.shape[0], dtype=jnp.int32)
    visible = places[None, :] <= places[:, None]
    scores = jnp.where(visible[None], scores, -1e+30)
    weights = jax.nn.softmax(scores, axis=-1)
    return jnp.einsum('hqk,khe->qhe', low(weights), values, precision=lax.Precision.HIGHEST)

def arrange(values):
    return values.reshape(N_SEQ, SEQS, SPAN, HEADS, HDIM).transpose(1, 0, 2, 3, 4).reshape(SEQS, N_SEQ * SPAN, HEADS, HDIM)

def restore(values):
    return values.reshape(SEQS, N_SEQ, SPAN, D).transpose(1, 0, 2, 3).reshape(TOKENS, D)

def one_layer(stream, gains, shifts, qkv_weight, qv_bias, out_weight, out_shift, fc_weight, fc_shift, proj_weight):
    normed = low(layer_norm(stream, gains[0], shifts[0]))
    qkv = dot_exact(normed, low(qkv_weight).reshape(D, 3 * D)).reshape(TOKENS, 3, D)
    query = low_back(low(qkv[:, 0] + qv_bias[0]))
    keys = low_back(low(qkv[:, 1]))
    values = low_back(low(qkv[:, 2] + qv_bias[1]))
    attended = lax.map(jax.checkpoint(attend_sequence), (arrange(query), arrange(keys), arrange(values)))
    merged = low_back(low(restore(attended)))
    residual = stream + low_back(dot_exact(merged, low(out_weight).T) + out_shift[0])
    normed_two = low(layer_norm(residual, gains[1], shifts[1]))
    pre_act = low_back(dot_exact(normed_two, low(fc_weight)) + fc_shift)
    inner = low(jax.nn.gelu(pre_act, approximate=True))
    return residual + low_back(dot_exact(inner, low(proj_weight).T) + out_shift[1])

def forward(tokens, norm_gain, norm_bias, w_qkv, b_qv, w_out, out_bias, w_fc, b_fc, w_proj):
    stream = tokens.T
    for layer_index in range(LAYERS):
        stream = one_layer(stream, norm_gain[layer_index], norm_bias[layer_index], w_qkv[layer_index], b_qv[layer_index], w_out[layer_index], out_bias[layer_index], w_fc[layer_index], b_fc[layer_index], w_proj[layer_index])
    return stream.T

def reference(tokens, cotangent, norm_gain, norm_bias, w_qkv, b_qv, w_out, out_bias, w_fc, b_fc, w_proj):
    stream_out, pullback = jax.vjp(forward, tokens, norm_gain, norm_bias, w_qkv, b_qv, w_out, out_bias, w_fc, b_fc, w_proj)
    grads = pullback(cotangent)
    return (stream_out, grads[0], grads[1], grads[2], grads[3], grads[4], grads[5], grads[6], grads[7], grads[8], grads[9])
```

```python
import functools
import math

import jax
import jax.numpy as jnp
from jax import lax
from jax.experimental import pallas as pl
from jax.experimental.pallas import tpu as pltpu
from jax.sharding import PartitionSpec as P

HEADS = 25
HDIM = 64
D = 1600
SPAN = 256
SLOTS = 4
PLANE = ("col", "row")

norm_eps = 1e-05
bf16 = jnp.bfloat16
f32 = jnp.float32


def dot_nn(left, right):
    return lax.dot_general(left, right, (((1,), (0,)), ((), ())), preferred_element_type=f32)


def dot_nt(left, right):
    return lax.dot_general(left, right, (((1,), (1,)), ((), ())), preferred_element_type=f32)


def dot_tn(left, right):
    return lax.dot_general(left, right, (((0,), (0,)), ((), ())), preferred_element_type=f32)


def swap_rows(values, split, concat):
    return lax.all_to_all(values, "row", split_axis=split, concat_axis=concat, tiled=True)


def plane_gather(values):
    return lax.all_gather(values, PLANE, axis=0, tiled=True)


def plane_sum(partial):
    return lax.psum_scatter(partial.astype(bf16), PLANE, scatter_dimension=0, tiled=True).astype(f32)


def partner_swap(values):
    count = lax.axis_size("row")
    return lax.ppermute(values, "row", [(low, low ^ 1) for low in range(count)])


def rows_to_heads(values):
    rows, parts, width = values.shape
    slots = lax.axis_size("seq") * 2 * SLOTS * HDIM
    values = jnp.pad(values, ((0, 0), (0, 0), (0, slots - width)))
    values = lax.all_to_all(values, "seq", split_axis=2, concat_axis=0, tiled=True)
    side = lax.axis_index("row") % 2
    half = SLOTS * HDIM
    own = lax.dynamic_slice_in_dim(values, side * half, half, 2)
    other = partner_swap(lax.dynamic_slice_in_dim(values, (1 - side) * half, half, 2))
    low = jnp.where(side == 0, own, other).reshape(-1, 1, rows, parts, half)
    high = jnp.where(side == 0, other, own).reshape(-1, 1, rows, parts, half)
    return jnp.concatenate([low, high], 1).reshape(-1, parts, half)


def heads_to_rows(values):
    positions, parts, half = values.shape
    count = lax.axis_size("seq")
    rows = positions // (2 * count)
    values = values.reshape(count, 2, rows, parts, half)
    side = lax.axis_index("row") % 2
    own = jnp.where(side == 0, values[:, 0], values[:, 1]).reshape(count * rows, parts, half)
    given = jnp.where(side == 0, values[:, 1], values[:, 0]).reshape(count * rows, parts, half)
    other = partner_swap(given)
    both = jnp.concatenate(
        [jnp.where(side == 0, own, other), jnp.where(side == 0, other, own)], 2
    )
    both = lax.all_to_all(both, "seq", split_axis=0, concat_axis=2, tiled=True)
    return both[:, :, :D]


def cols_to_rows(values):
    return lax.all_to_all(values, PLANE, split_axis=0, concat_axis=2, tiled=True)


def rows_to_cols(values):
    return lax.all_to_all(values, PLANE, split_axis=2, concat_axis=0, tiled=True)


def sum_weights(grad, own_shape):
    rows, cols = lax.axis_size("row"), lax.axis_size("seq")
    width = grad.shape[-1]
    split = grad.astype(bf16).reshape(rows, cols, -1, width)
    split = lax.psum_scatter(split, "seq", scatter_dimension=1, tiled=True)[:, 0]
    split = lax.all_to_all(split, "row", split_axis=0, concat_axis=0, tiled=True)
    return lax.all_gather(split, "seq", axis=0, tiled=False)


def masked_scores(query, keys, block):
    scores = dot_nt(query, keys)
    rows, width = scores.shape
    row_at = lax.broadcasted_iota(jnp.int32, (rows, width), 0) + block * rows
    col_at = lax.broadcasted_iota(jnp.int32, (rows, width), 1)
    return jnp.where(col_at <= row_at, scores, -1e30)


def softmax_rows(scores):
    weights = jnp.exp(scores - jnp.max(scores, 1, keepdims=True))
    return weights * (1.0 / jnp.sum(weights, 1, keepdims=True))


def attend_kernel(q_ref, k_ref, v_ref, out_ref):
    blocks = q_ref.shape[0] // SPAN
    for block in range(blocks):
        rows = slice(block * SPAN, (block + 1) * SPAN)
        seen = slice(0, (block + 1) * SPAN)
        parts = []
        for head in range(2):
            cols = slice(head * HDIM, (head + 1) * HDIM)
            query = q_ref[rows, cols] * bf16(HDIM**-0.5)
            weights = softmax_rows(masked_scores(query, k_ref[seen, cols], block))
            parts.append(dot_nn(weights.astype(bf16), v_ref[seen, cols]))
        out_ref[rows, :] = jnp.concatenate(parts, 1).astype(bf16)


def attend_back_kernel(q_ref, k_ref, v_ref, da_ref, dq_ref, dk_ref, dv_ref, dk_sum, dv_sum):
    blocks = q_ref.shape[0] // SPAN
    dk_sum[...] = jnp.zeros_like(dk_sum)
    dv_sum[...] = jnp.zeros_like(dv_sum)
    for block in range(blocks):
        rows = slice(block * SPAN, (block + 1) * SPAN)
        seen = slice(0, (block + 1) * SPAN)
        dq_parts, dk_parts, dv_parts = [], [], []
        for head in range(2):
            cols = slice(head * HDIM, (head + 1) * HDIM)
            query = q_ref[rows, cols] * bf16(HDIM**-0.5)
            keys, grad = k_ref[seen, cols], da_ref[rows, cols]
            weights = softmax_rows(masked_scores(query, keys, block))
            grad_weights = dot_nt(grad, v_ref[seen, cols])
            along = jnp.sum(grad_weights * weights, 1, keepdims=True)
            grad_scores = (weights * (grad_weights - along)).astype(bf16)
            dq_parts.append(dot_nn(grad_scores, keys) * HDIM**-0.5)
            dk_parts.append(dot_tn(grad_scores, query))
            dv_parts.append(dot_tn(weights.astype(bf16), grad))
        dq_ref[rows, :] = jnp.concatenate(dq_parts, 1).astype(bf16)
        dk_sum[seen, :] += jnp.concatenate(dk_parts, 1)
        dv_sum[seen, :] += jnp.concatenate(dv_parts, 1)
    dk_ref[...] = dk_sum[...].astype(bf16)
    dv_ref[...] = dv_sum[...].astype(bf16)


def attend(qkv):
    positions = qkv.shape[0]
    pairs = SLOTS // 2
    flat = qkv.reshape(positions, 3 * SLOTS * HDIM)
    spec = lambda part: pl.BlockSpec((positions, 2 * HDIM), lambda i: (0, part * pairs + i))
    return pl.pallas_call(
        attend_kernel,
        grid=(pairs,),
        in_specs=[spec(0), spec(1), spec(2)],
        out_specs=spec(0),
        out_shape=jax.ShapeDtypeStruct((positions, SLOTS * HDIM), bf16),
        compiler_params=pltpu.CompilerParams(vmem_limit_bytes=48 << 20),
        name="attend",
    )(flat, flat, flat)


def attend_back(qkv, grad):
    positions = qkv.shape[0]
    pairs = SLOTS // 2
    flat = qkv.reshape(positions, 3 * SLOTS * HDIM)
    spec = lambda part: pl.BlockSpec((positions, 2 * HDIM), lambda i: (0, part * pairs + i))
    shape = jax.ShapeDtypeStruct((positions, SLOTS * HDIM), bf16)
    grads = pl.pallas_call(
        attend_back_kernel,
        grid=(pairs,),
        in_specs=[spec(0), spec(1), spec(2), spec(0)],
        out_specs=[spec(0)] * 3,
        out_shape=[shape] * 3,
        scratch_shapes=[pltpu.VMEM((positions, 2 * HDIM), f32)] * 2,
        compiler_params=pltpu.CompilerParams(vmem_limit_bytes=48 << 20),
        name="attend_back",
    )(flat, flat, flat, grad)
    return jnp.stack(grads, 1)


def norm_forward(stream, gain, shift):
    mean_value = jnp.mean(stream, 1, keepdims=True)
    centred = stream - mean_value
    inverse = lax.rsqrt(jnp.mean(centred * centred, 1, keepdims=True) + norm_eps)
    normal_part = centred * inverse
    return ((normal_part * gain + shift).astype(bf16), normal_part, inverse)


def norm_backward(grad_out, normal_part, inverse, gain):
    scaled = grad_out * gain
    grad_in = inverse * (
        scaled
        - jnp.mean(scaled, 1, keepdims=True)
        - normal_part * jnp.mean(scaled * normal_part, 1, keepdims=True)
    )
    return (grad_in, jnp.sum(grad_out * normal_part, 0), jnp.sum(grad_out, 0))


def activation(values):
    return jax.nn.gelu(values, approximate=True)


def activation_grad(values, grad_values):
    unused_value, pullback = jax.vjp(activation, values)
    return pullback(grad_values)[0]


def per_device_any(
    tokens, cotangent, norm_gain, norm_bias, w_qkv, b_qv, w_out, out_bias, w_fc, b_fc, w_proj
):
    layers = w_qkv.shape[0]
    row_width = tokens.shape[0]
    col_width = w_out.shape[2]
    ff_width = w_fc.shape[2]
    n_rows, row = lax.axis_size("row"), lax.axis_index("row")
    own_cols, own_ff = col_width // n_rows, ff_width // n_rows

    vectors = jnp.stack([norm_gain, norm_bias, out_bias])
    vectors = lax.all_gather(vectors, "row", axis=3, tiled=True)
    gains, shifts, out_shifts = vectors[0], vectors[1], vectors[2]
    qv_bias = lax.dynamic_slice_in_dim(b_qv, row * own_cols, own_cols, 2)
    fc_bias = lax.dynamic_slice_in_dim(b_fc, row * own_ff, own_ff, 1)

    stream = swap_rows(tokens, 1, 0).T
    weights = []
    for layer in range(layers):
        qkv_matrix = swap_rows(w_qkv[layer].astype(bf16), 2, 0).reshape(D, 3 * own_cols)
        out_matrix = lax.all_gather(w_out[layer].astype(bf16), "row", axis=0, tiled=True)
        out_matrix = lax.all_gather(out_matrix, "col", axis=1, tiled=True)
        fc_matrix = swap_rows(w_fc[layer].astype(bf16), 1, 0)
        proj_matrix = swap_rows(w_proj[layer].astype(bf16), 1, 0)
        weights.append((qkv_matrix, out_matrix, fc_matrix, proj_matrix))
    saved = []
    for layer in range(layers):
        qkv_matrix, out_matrix, fc_matrix, proj_matrix = weights[layer]
        normed, normal_one, inverse_one = norm_forward(stream, gains[layer, 0], shifts[layer, 0])
        all_one = plane_gather(normed)
        bias = jnp.concatenate(
            [qv_bias[layer, 0], jnp.zeros_like(qv_bias[layer, 0]), qv_bias[layer, 1]]
        )
        qkv_cols = (dot_nn(all_one, qkv_matrix) + bias).astype(bf16)
        qkv = rows_to_heads(cols_to_rows(qkv_cols.reshape(-1, 3, own_cols)))
        attended = heads_to_rows(attend(qkv)[:, None])
        att_cols = rows_to_cols(attended)[:, 0]
        attended = attended[:, 0]
        residual = stream + (dot_nt(attended, out_matrix) + out_shifts[layer, 0])
        normed, normal_two, inverse_two = norm_forward(residual, gains[layer, 1], shifts[layer, 1])
        all_two = plane_gather(normed)
        pre_act = dot_nn(all_two, fc_matrix) + fc_bias[layer]
        act = activation(pre_act).astype(bf16)
        stream = residual + (plane_sum(dot_nt(act, proj_matrix)) + out_shifts[layer, 1])
        saved.append(
            (all_one, normal_one, inverse_one, qkv, att_cols, all_two, normal_two, inverse_two, pre_act, act)
        )
    grad_stream = swap_rows(cotangent, 1, 0).T
    grads = [None] * layers
    vector_grads = [None] * layers
    for layer in reversed(range(layers)):
        qkv_matrix, out_matrix, fc_matrix, proj_matrix = weights[layer]
        all_one, normal_one, inverse_one, qkv, att_cols, all_two, normal_two, inverse_two, pre_act, act = saved[layer]
        grad_low = grad_stream.astype(bf16)
        proj_shift = jnp.sum(grad_low.astype(f32), 0)
        all_grad = plane_gather(grad_low)
        proj_grad = sum_weights(dot_tn(all_grad, act), w_proj.shape[1:])
        grad_pre = activation_grad(pre_act, dot_nn(all_grad, proj_matrix)).astype(bf16)
        fc_grad = sum_weights(dot_tn(all_two, grad_pre), w_fc.shape[1:])
        fc_shift = jnp.sum(grad_pre.astype(f32), 0)
        grad_normed = plane_sum(dot_nt(grad_pre, fc_matrix))
        grad_in, gain_two, shift_two = norm_backward(grad_normed, normal_two, inverse_two, gains[layer, 1])
        grad_res = grad_stream + grad_in
        grad_low = grad_res.astype(bf16)
        out_shift = jnp.sum(grad_low.astype(f32), 0)
        grad_att = dot_nn(grad_low, out_matrix).astype(bf16)
        out_grad = sum_weights(dot_tn(plane_gather(grad_low), att_cols), w_out.shape[1:])
        grad_heads = rows_to_heads(grad_att[:, None])[:, 0]
        grad_rows = heads_to_rows(attend_back(qkv, grad_heads))
        grad_cols = rows_to_cols(grad_rows).reshape(-1, 3 * own_cols)
        qkv_grad = sum_weights(dot_tn(all_one, grad_cols), w_qkv.shape[1:])
        bias_sums = jnp.sum(grad_cols.astype(f32), 0).reshape(3, own_cols)
        grad_normed = plane_sum(dot_nt(grad_cols, qkv_matrix))
        grad_in, gain_one, shift_one = norm_backward(grad_normed, normal_one, inverse_one, gains[layer, 0])
        grad_stream = grad_res + grad_in
        grads[layer] = (qkv_grad, out_grad, fc_grad, proj_grad)
        vector_grads[layer] = (
            jnp.stack([jnp.stack([gain_one, gain_two]), jnp.stack([shift_one, shift_two]), jnp.stack([out_shift, proj_shift])]),
            jnp.stack([bias_sums[0], bias_sums[2]]),
            fc_shift,
        )
    wide = lax.psum(jnp.stack([v[0] for v in vector_grads]), ("seq", "col", "row"))
    wide = lax.dynamic_slice_in_dim(wide, row * row_width, row_width, 3)
    slim = jnp.concatenate(
        [jnp.concatenate([v[1].reshape(2, own_cols), v[2].reshape(ff_width // col_width, own_cols)]) for v in vector_grads]
    ).reshape(layers, -1, own_cols)
    slim_qv = lax.psum(jnp.stack([v[1] for v in vector_grads]), "seq")
    slim_fc = lax.psum(jnp.stack([v[2] for v in vector_grads]), "seq")
    qv_total = lax.all_gather(slim_qv, "row", axis=2, tiled=True)
    fc_total = lax.all_gather(slim_fc, "row", axis=1, tiled=True)

    def as_grid(member, shape):
        done = []
        for layer in range(layers):
            blocks = grads[layer][member]
            n_seq, parts = blocks.shape[:2]
            if len(shape) == 3:
                blocks = blocks.reshape(n_seq, parts, -1, 3, own_cols).transpose(0, 2, 3, 1, 4)
            else:
                blocks = blocks.transpose(0, 2, 1, 3)
            done.append(blocks.reshape(shape).astype(f32))
        return jnp.stack(done)

    return (
        swap_rows(stream.T, 0, 1),
        swap_rows(grad_stream.T, 0, 1),
        wide[:, 0],
        wide[:, 1],
        as_grid(0, w_qkv.shape[1:]),
        qv_total,
        as_grid(1, w_out.shape[1:]),
        wide[:, 2],
        as_grid(2, w_fc.shape[1:]),
        fc_total,
        as_grid(3, w_proj.shape[1:]),
    )


MESH = pl.DeviceIdType.MESH
DMA = pltpu.SemaphoreType.DMA
BLOCK = 128
WIN = SLOTS * HDIM
VMEM = pltpu.VMEM
STEP = 3 * HDIM


def place():
    col, row = lax.axis_index("col"), lax.axis_index("row")
    flip = col + 1 - 2 * lax.rem(col, 2)
    far = lax.rem(col + 2, 4)
    cross = lax.rem(flip + 2, 4)
    return col, flip, far, cross, row, 1 - row


def greet(along_seq):
    col, flip, far, cross, row, other = place()
    barrier = pltpu.get_barrier_semaphore()
    partners = [{"col": flip}, {"row": other}, {"col": far}]
    if along_seq:
        here = lax.axis_index("seq")
        partners += [{"seq": lax.rem(here + step, 4)} for step in (1, 2, 3)]
    for partner in partners:
        pl.semaphore_signal(barrier, inc=1, device_id=partner, device_id_type=MESH)
    pl.semaphore_wait(barrier, len(partners))


def remote(src, dst, send, recv, index, device):
    return pltpu.make_async_remote_copy(
        src_ref=src,
        dst_ref=dst,
        send_sem=send.at[index],
        recv_sem=recv.at[index],
        device_id=device,
        device_id_type=MESH,
    )


GATHER_SCRATCH = [DMA((10,)), DMA((10,))]


def gather(full, send, recv, body):
    col, flip, far, cross, row, other = place()
    half = BLOCK // 2
    low, high = pl.ds(0, half), pl.ds(half, half)
    core, along_x, along_y = {"col": flip}, {"row": other}, {"col": far}

    def copy(index, ref, device):
        return remote(ref, ref, send, recv, index, device)

    copies = [
        copy(0, full.at[col, row], core),
        copy(1, full.at[col, row, low], along_x),
        copy(2, full.at[col, row, high], along_y),
        copy(3, full.at[col, row, high], along_x),
        copy(4, full.at[col, row, low], along_y),
        copy(5, full.at[col, other, low], along_y),
        copy(6, full.at[far, row, high], along_x),
        copy(7, full.at[col, other], core),
        copy(8, full.at[far, row], core),
        copy(9, full.at[far, other], core),
    ]
    for index in (1, 2, 0, 3, 4):
        copies[index].start()
    for arrived, started in ((1, 5), (2, 6), (3, 7), (4, 8)):
        copies[arrived].wait_recv()
        copies[started].start()
    body(col)
    copies[5].wait_recv()
    copies[6].wait_recv()
    copies[9].start()
    copies[0].wait_recv()
    copies[7].wait_recv()
    body(flip)
    body(far)
    copies[8].wait_recv()
    copies[9].wait_recv()
    body(cross)
    for each in copies:
        each.wait_send()


SCATTER_SCRATCH = [
    VMEM((2, 2, BLOCK, D), bf16),
    VMEM((2, 2, BLOCK, D), bf16),
    VMEM((2, 2, BLOCK, D), bf16),
    VMEM((2, BLOCK, D), f32),
    VMEM((3, BLOCK // 2, D), bf16),
    VMEM((3, BLOCK // 2, D), bf16),
    VMEM((2, BLOCK // 2, D), bf16),
    DMA((8,)),
    DMA((8,)),
]


def scatter(compute, given, taken, part, own, from_x, from_y, turn, send, recv):
    col, flip, far, cross, row, other = place()
    half = BLOCK // 2
    low, high = pl.ds(0, half), pl.ds(half, half)
    core, along_x, along_y = {"col": flip}, {"row": other}, {"col": far}

    def copy(index, src, dst, device):
        return remote(src, dst, send, recv, index, device)

    sib_own = copy(0, given.at[1], taken.at[1], core)
    sib_far = copy(1, given.at[0], taken.at[0], core)
    x_far = copy(2, part.at[0, other, low], from_x.at[1], along_x)
    y_far = copy(3, part.at[0, other, high], from_y.at[1], along_y)
    y_own = copy(4, part.at[0, row, high], from_y.at[0], along_y)
    x_own = copy(5, part.at[1, other, low], from_x.at[0], along_x)
    y_turn = copy(6, turn.at[0], from_y.at[2], along_y)
    x_turn = copy(7, turn.at[1], from_x.at[2], along_x)
    shape = (2, BLOCK, D)
    given[1] = compute(flip).reshape(shape).astype(bf16)
    sib_own.start()
    given[0] = compute(cross).reshape(shape).astype(bf16)
    sib_far.start()
    value = compute(far).reshape(shape)
    sib_far.wait_recv()
    part[0] = (value + taken[0].astype(f32)).astype(bf16)
    x_far.start()
    y_far.start()
    y_own.start()
    value = compute(col).reshape(shape)
    sib_own.wait_recv()
    own[...] = value + taken[1].astype(f32)
    part[1] = own[...].astype(bf16)
    x_own.start()
    x_far.wait_recv()
    turn[0] = (part[0, row, low].astype(f32) + from_x[1].astype(f32)).astype(bf16)
    y_turn.start()
    y_far.wait_recv()
    turn[1] = (own[other, high] + from_y[1].astype(f32)).astype(bf16)
    x_turn.start()
    x_own.wait_recv()
    y_own.wait_recv()
    y_turn.wait_recv()
    x_turn.wait_recv()
    total = jnp.concatenate(
        [
            own[row, low] + from_x[0].astype(f32) + from_y[2].astype(f32),
            own[row, high] + from_y[0].astype(f32) + from_x[2].astype(f32),
        ],
        0,
    )
    for each in (sib_own, sib_far, x_far, y_far, y_own, x_own, y_turn, x_turn):
        each.wait_send()
    return total


SEQ_SCRATCH = [DMA((4,)), DMA((4,))]


def seq_copy(src, dst, send, recv, group):
    here = lax.axis_index("seq")
    return pltpu.make_async_remote_copy(
        src_ref=src.at[group],
        dst_ref=dst.at[here],
        send_sem=send.at[group],
        recv_sem=recv.at[here],
        device_id={"seq": group},
        device_id_type=MESH,
    )


def seq_send(src, dst, send, recv, group):
    here = lax.axis_index("seq")

    @pl.when(group != here)
    def _():
        seq_copy(src, dst, send, recv, group).start()

    @pl.when(group == here)
    def _():
        dst[here] = src[here]


def seq_wait(src, dst, send, recv, group):
    @pl.when(group != lax.axis_index("seq"))
    def _():
        pltpu.make_async_remote_copy(
            src_ref=src.at[group],
            dst_ref=dst.at[group],
            send_sem=send.at[group],
            recv_sem=recv.at[group],
            device_id={"seq": group},
            device_id_type=MESH,
        ).wait_recv()


def seq_sent(src, dst, send, recv):
    for group in range(4):

        @pl.when(group != lax.axis_index("seq"))
        def _():
            seq_copy(src, dst, send, recv, group).wait_send()


def norm_rows(stream):
    mean_value = jnp.mean(stream, 1, keepdims=True)
    centred = stream - mean_value
    inverse = lax.rsqrt(jnp.mean(centred * centred, 1, keepdims=True) + norm_eps)
    return centred * inverse, inverse


def attention_forward(
    stream, gain, shift, w_hbm, bias, full, heads, att,
    w, qkv, sent, w_sem, g_send, g_recv, q_send, q_recv, a_send, a_recv,
):
    col, flip, far, cross, row, other = place()
    weights = pltpu.make_async_copy(w_hbm, w, w_sem)
    weights.start()
    greet(True)
    normal_part, unused = norm_rows(stream[...])
    full[col, row] = (normal_part * gain[...] + shift[...]).astype(bf16)
    seen = []

    def project(group):
        if not seen:
            weights.wait()
        seen.append(0)
        rows = full[group].reshape(2 * BLOCK, D)
        qkv[group] = (dot_nn(rows, w[...]) + bias[...]).astype(bf16)
        seq_send(qkv, heads, q_send, q_recv, group)

    gather(full, g_send, g_recv, project)
    for block in range(4):
        seq_wait(qkv, heads, q_send, q_recv, block)
        keys_seen = (block + 1) * SPAN
        for pair in range(SLOTS // 2):
            parts = []
            for head in range(2):
                low = (2 * pair + head) * HDIM
                query = heads[block, :, low : low + HDIM] * bf16(HDIM**-0.5)
                keys = heads[: block + 1, :, WIN + low : WIN + low + HDIM].reshape(keys_seen, HDIM)
                values = heads[: block + 1, :, 2 * WIN + low : 2 * WIN + low + HDIM].reshape(keys_seen, HDIM)
                p = softmax_rows(masked_scores(query, keys, block)).astype(bf16)
                parts.append(dot_nn(p, values))
            sent[block, :, 2 * pair * HDIM : 2 * (pair + 1) * HDIM] = jnp.concatenate(parts, 1).astype(bf16)
        seq_send(sent, att, a_send, a_recv, block)
    for block in range(4):
        seq_wait(sent, att, a_send, a_recv, block)
    seq_sent(qkv, heads, q_send, q_recv)
    seq_sent(sent, att, a_send, a_recv)


def gelu_terms(values):
    k = math.sqrt(2 / math.pi)
    squares = values * values
    t = jnp.tanh(values * (k + (k * 0.044715) * squares))
    return t, squares


def mlp_forward(
    att, stream, w_out, out_shift, gain, shift, fc_hbm, fc_bias, proj_hbm, proj_shift,
    res, full, pre, act, result,
    fc, proj, w_sem, g_send, g_recv, *scratch,
):
    col, flip, far, cross, row, other = place()
    fc_copy = pltpu.make_async_copy(fc_hbm, fc, w_sem.at[0])
    proj_copy = pltpu.make_async_copy(proj_hbm, proj, w_sem.at[1])
    fc_copy.start()
    proj_copy.start()
    greet(False)
    count = len(SCATTER_SCRATCH)
    total = scatter(lambda group: dot_nt(att[group], w_out[...]), *scratch[:count])
    res[...] = stream[...] + (total + out_shift[...])
    normal_part, unused = norm_rows(res[...])
    full[col, row] = (normal_part * gain[...] + shift[...]).astype(bf16)
    seen = []

    def widen(group):
        if not seen:
            fc_copy.wait()
        seen.append(0)
        u = dot_nn(full[group].reshape(2 * BLOCK, D), fc[...]) + fc_bias[...]
        pre[group] = u
        t, unused = gelu_terms(u)
        act[group] = (0.5 * u * (1 + t)).astype(bf16)

    gather(full, g_send, g_recv, widen)
    proj_copy.wait()
    total = scatter(lambda group: dot_nt(act[group], proj[...]), *scratch[count:])
    result[...] = res[...] + (total + proj_shift[...])


def norm_back_rows(grad_out, normal_part, inverse, gain):
    scaled = grad_out * gain
    return inverse * (
        scaled
        - jnp.mean(scaled, 1, keepdims=True)
        - normal_part * jnp.mean(scaled * normal_part, 1, keepdims=True)
    )


def mlp_backward(
    grad, res, gain, pre_hbm, fc_hbm, proj_hbm, w_out,
    full, grad_pre, full_res, grad_res, grad_att, sums,
    fc, proj, pre, w_sem, g_send, g_recv, h_send, h_recv, *scratch,
):
    col, flip, far, cross, row, other = place()
    proj_copy = pltpu.make_async_copy(proj_hbm, proj, w_sem.at[0])
    pre_copy = pltpu.make_async_copy(pre_hbm, pre, w_sem.at[1])
    fc_copy = pltpu.make_async_copy(fc_hbm, fc, w_sem.at[2])
    proj_copy.start()
    pre_copy.start()
    fc_copy.start()
    greet(False)
    low = grad[...].astype(bf16)
    full[col, row] = low
    sums[0:1, :] = jnp.sum(low.astype(f32), 0, keepdims=True)
    seen = []

    def widen(group):
        if not seen:
            proj_copy.wait()
            pre_copy.wait()
        seen.append(0)
        grad_act = dot_nn(full[group].reshape(2 * BLOCK, D), proj[...])
        u = pre[group]
        t, squares = gelu_terms(u)
        k = math.sqrt(2 / math.pi)
        slope = 0.5 * (1 + t) + 0.5 * u * (1 - t * t) * (k + (3 * k * 0.044715) * squares)
        grad_pre[group] = (grad_act * slope).astype(bf16)

    gather(full, g_send, g_recv, widen)
    fc_copy.wait()
    total = scatter(lambda group: dot_nt(grad_pre[group], fc[...]), *scratch)
    normal_part, inverse = norm_rows(res[...])
    sums[1:2, :] = jnp.sum(total * normal_part, 0, keepdims=True)
    sums[2:3, :] = jnp.sum(total, 0, keepdims=True)
    grad_res[...] = grad[...] + norm_back_rows(total, normal_part, inverse, gain[...])
    low = grad_res[...].astype(bf16)
    full_res[col, row] = low
    sums[3:4, :] = jnp.sum(low.astype(f32), 0, keepdims=True)
    sums[4:8, :] = jnp.zeros((4, D), f32)

    def out_back(group):
        grad_att[group] = dot_nn(full_res[group].reshape(2 * BLOCK, D), w_out[...]).astype(bf16)

    gather(full_res, h_send, h_recv, out_back)


def attention_backward(
    heads, grad_att, grad_res, stream, gain, w_hbm,
    grad_qkv, result, sums,
    w, da, dk, dv, sent, w_sem, a_send, a_recv, q_send, q_recv, *scratch,
):
    weights = pltpu.make_async_copy(w_hbm, w, w_sem)
    weights.start()
    greet(True)
    for group in range(4):
        seq_send(grad_att, da, a_send, a_recv, group)
    for block in (3, 2, 1, 0):
        seq_wait(grad_att, da, a_send, a_recv, block)
        keys_seen = (block + 1) * SPAN
        for pair in range(SLOTS // 2):
            dq_parts, dk_parts, dv_parts = [], [], []
            for head in range(2):
                low = (2 * pair + head) * HDIM
                query = heads[block, :, low : low + HDIM] * bf16(HDIM**-0.5)
                keys = heads[: block + 1, :, WIN + low : WIN + low + HDIM].reshape(keys_seen, HDIM)
                values = heads[: block + 1, :, 2 * WIN + low : 2 * WIN + low + HDIM].reshape(keys_seen, HDIM)
                grad = da[block, :, low : low + HDIM]
                p = softmax_rows(masked_scores(query, keys, block))
                dp = dot_nt(grad, values)
                ds = (p * (dp - jnp.sum(dp * p, 1, keepdims=True))).astype(bf16)
                dq_parts.append(dot_nn(ds, keys) * HDIM**-0.5)
                dk_parts.append(dot_tn(ds, query))
                dv_parts.append(dot_tn(p.astype(bf16), grad))
            cols = slice(2 * pair * HDIM, 2 * (pair + 1) * HDIM)
            new_dk = jnp.concatenate(dk_parts, 1).reshape(block + 1, SPAN, 2 * HDIM)
            new_dv = jnp.concatenate(dv_parts, 1).reshape(block + 1, SPAN, 2 * HDIM)
            if block < 3:
                new_dk = new_dk + dk[: block + 1, :, cols]
                new_dv = new_dv + dv[: block + 1, :, cols]
            dk[: block + 1, :, cols] = new_dk
            dv[: block + 1, :, cols] = new_dv
            sent[block, :, cols] = jnp.concatenate(dq_parts, 1).astype(bf16)
        sent[block, :, WIN : 2 * WIN] = dk[block].astype(bf16)
        sent[block, :, 2 * WIN :] = dv[block].astype(bf16)
        seq_send(sent, grad_qkv, q_send, q_recv, block)
    weights.wait()
    for block in range(4):
        seq_wait(sent, grad_qkv, q_send, q_recv, block)
    total = scatter(lambda group: dot_nt(grad_qkv[group], w[...]), *scratch)
    normal_part, inverse = norm_rows(stream[...])
    sums[0:1, :] = jnp.sum(total * normal_part, 0, keepdims=True)
    sums[1:2, :] = jnp.sum(total, 0, keepdims=True)
    sums[2:8, :] = jnp.zeros((6, D), f32)
    result[...] = grad_res[...] + norm_back_rows(total, normal_part, inverse, gain[...])
    seq_sent(grad_att, da, a_send, a_recv)
    seq_sent(sent, grad_qkv, q_send, q_recv)


def call(kernel, ident, places, outs, scratch, cost, *operands):
    spaces = {"v": VMEM, "h": pl.ANY}
    return pl.pallas_call(
        kernel,
        in_specs=[pl.BlockSpec(memory_space=spaces[each]) for each in places],
        out_specs=[pl.BlockSpec(memory_space=VMEM)] * len(outs),
        out_shape=[jax.ShapeDtypeStruct(shape, kind) for shape, kind in outs],
        scratch_shapes=scratch,
        compiler_params=pltpu.CompilerParams(
            collective_id=ident, has_side_effects=True, vmem_limit_bytes=60 << 20
        ),
        cost_estimate=pl.CostEstimate(flops=cost, bytes_accessed=0, transcendentals=0),
        name=kernel.__name__,
    )(*operands)


def partner_halves(own, given, axis):
    row = lax.axis_index("row")
    other = partner_swap(given)
    return jnp.concatenate(
        [jnp.where(row == 0, own, other), jnp.where(row == 0, other, own)], axis
    )


def ff_columns(block):
    width = block.shape[1] // 2
    row = lax.axis_index("row")
    own = lax.dynamic_slice_in_dim(block, row * width, width, 1)
    given = lax.dynamic_slice_in_dim(block, (1 - row) * width, width, 1)
    return partner_halves(own, given, 0)


def head_columns(block):
    col, row = lax.axis_index("col"), lax.axis_index("row")
    edge = 3 * 16
    left = lax.ppermute(block[..., -edge:], "col", [(0, 1), (1, 2), (2, 3)])
    wide = jnp.concatenate([left, block, jnp.zeros_like(block[..., :edge])], -1)
    start = edge - 16 * col
    own = lax.dynamic_slice_in_dim(wide, start + row * STEP, WIN, 2)
    given = lax.dynamic_slice_in_dim(wide, start + (1 - row) * STEP, WIN, 2)
    return partner_halves(own, given, 0)


def summed_quarter(grad):
    split = grad.astype(bf16).reshape(2, 4, D // 8, -1).transpose(1, 0, 2, 3)
    return lax.psum_scatter(split, "seq", scatter_dimension=0, tiled=True)[0]


def swapped_quarter(split):
    row = lax.axis_index("row")
    own = lax.dynamic_index_in_dim(split, row, 0, False)
    given = lax.dynamic_index_in_dim(split, 1 - row, 0, False)
    other = partner_swap(given)
    return jnp.where(row == 0, own, other), jnp.where(row == 0, other, own)


def ff_block(split):
    first, second = swapped_quarter(split)
    return lax.all_gather(jnp.concatenate([first, second], 1), "seq", axis=0, tiled=True)


def head_block(split, parts):
    col = lax.axis_index("col")
    first, second = swapped_quarter(split)
    first, second = first.reshape(-1, parts, WIN), second.reshape(-1, parts, WIN)
    after = lax.ppermute(first[..., :HDIM], "col", [(1, 0), (2, 1), (3, 2)])
    tail = jnp.where(col == 3, second[..., STEP:], after)
    wide = jnp.concatenate([first[..., :STEP], second[..., :STEP], tail], -1)
    block = lax.dynamic_slice_in_dim(wide, 16 * col, 400, 2)
    return lax.all_gather(block, "seq", axis=0, tiled=True)


def per_device_plane(
    tokens, cotangent, norm_gain, norm_bias, w_qkv, b_qv, w_out, out_bias, w_fc, b_fc, w_proj
):
    layers = w_qkv.shape[0]
    half_d = tokens.shape[0]
    ff = w_fc.shape[2] // 2
    row, col = lax.axis_index("row"), lax.axis_index("col")
    device = 2 * col + row

    vectors = jnp.stack([norm_gain, norm_bias, out_bias])
    vectors = lax.all_gather(vectors, "row", axis=3, tiled=True)
    gains, shifts, out_shifts = vectors[0], vectors[1], vectors[2]
    fc_bias = lax.dynamic_slice_in_dim(b_fc, row * ff, ff, 1)
    qv_bias = lax.all_gather(b_qv, "col", axis=2, tiled=True)
    qv_bias = lax.dynamic_slice_in_dim(jnp.pad(qv_bias, ((0, 0), (0, 0), (0, HDIM))), STEP * device, WIN, 2)
    qkv_bias = jnp.concatenate([qv_bias[:, 0], jnp.zeros_like(qv_bias[:, 0]), qv_bias[:, 1]], 1)
    kept = (jnp.arange(WIN) < STEP) | (device == 7)

    def own_rows(columns):
        width = columns.shape[1] // 2
        own = lax.dynamic_slice_in_dim(columns, row * width, width, 1)
        given = lax.dynamic_slice_in_dim(columns, (1 - row) * width, width, 1)
        return partner_halves(own, given, 0).T

    def own_columns(rows):
        columns = rows.T
        own = lax.dynamic_slice_in_dim(columns, row * half_d, half_d, 0)
        given = lax.dynamic_slice_in_dim(columns, (1 - row) * half_d, half_d, 0)
        return partner_halves(own, given, 1)

    stream = own_rows(tokens)
    weights = []
    for layer in range(layers):
        qkv_matrix = head_columns(w_qkv[layer].astype(bf16)).reshape(D, 3 * WIN)
        out_matrix = head_columns(w_out[layer].astype(bf16)[:, None])[:, 0]
        out_matrix = jnp.where(kept[None], out_matrix, jnp.zeros_like(out_matrix))
        weights.append((qkv_matrix, out_matrix, ff_columns(w_fc[layer].astype(bf16)), ff_columns(w_proj[layer].astype(bf16))))

    full_shape = ((4, 2, BLOCK, D), bf16)
    rows_shape = ((BLOCK, D), f32)
    group = lambda width, kind: ((4, 2 * BLOCK, width), kind)
    matrix = lambda width: VMEM((D, width), bf16)
    work = lambda width: 2 * 8 * BLOCK * D * width
    saved = []
    for layer in range(layers):
        qkv_matrix, out_matrix, fc_matrix, proj_matrix = weights[layer]
        all_one, heads, att = call(
            attention_forward, 1, "vvvhv",
            [full_shape, group(3 * WIN, bf16), group(WIN, bf16)],
            [matrix(3 * WIN), VMEM(*group(3 * WIN, bf16)), VMEM(*group(WIN, bf16)), DMA] + GATHER_SCRATCH + 2 * SEQ_SCRATCH,
            4 * work(3 * WIN),
            stream, gains[layer, :1], shifts[layer, :1], qkv_matrix, qkv_bias[layer][None],
        )
        res, all_two, pre, act, result = call(
            mlp_forward, 2, "vvvvvvhvhv",
            [rows_shape, full_shape, group(ff, f32), group(ff, bf16), rows_shape],
            [matrix(ff), matrix(ff), DMA((2,))] + GATHER_SCRATCH + 2 * SCATTER_SCRATCH,
            2 * work(ff) + work(WIN),
            att, stream, out_matrix, out_shifts[layer, :1], gains[layer, 1:], shifts[layer, 1:],
            fc_matrix, fc_bias[layer][None], proj_matrix, out_shifts[layer, 1:],
        )
        saved.append((stream, all_one, heads, att, res, all_two, pre, act))
        stream = result
    grad = own_rows(cotangent)
    grads, vector_grads = [None] * layers, [None] * layers
    for layer in reversed(range(layers)):
        qkv_matrix, out_matrix, fc_matrix, proj_matrix = weights[layer]
        before, all_one, heads, att, res, all_two, pre, act = saved[layer]
        all_grad, grad_pre, all_res, grad_res, grad_att, sums = call(
            mlp_backward, 3, "vvvhhhv",
            [full_shape, group(ff, bf16), full_shape, rows_shape, group(WIN, bf16), ((8, D), f32)],
            [matrix(ff), matrix(ff), VMEM(*group(ff, f32)), DMA((3,))] + 2 * GATHER_SCRATCH + SCATTER_SCRATCH,
            2 * work(ff) + work(WIN),
            grad, res, gains[layer, 1:], pre, fc_matrix, proj_matrix, out_matrix,
        )
        grad_qkv, grad, more_sums = call(
            attention_backward, 4, "vvvvvh",
            [group(3 * WIN, bf16), rows_shape, ((8, D), f32)],
            [matrix(3 * WIN), VMEM(*group(WIN, bf16)), VMEM(*group(WIN, f32)), VMEM(*group(WIN, f32)), VMEM(*group(3 * WIN, bf16)), DMA]
            + 2 * SEQ_SCRATCH + SCATTER_SCRATCH,
            4 * work(3 * WIN),
            heads, grad_att, grad_res, before, gains[layer, :1], qkv_matrix,
        )
        rows = lambda values: values.reshape(8 * BLOCK, -1)
        proj_grad = dot_tn(rows(all_grad), rows(act))
        fc_grad = dot_tn(rows(all_two), rows(grad_pre))
        out_grad = dot_tn(rows(all_res), rows(att))
        qkv_grad = dot_tn(rows(all_one), rows(grad_qkv))
        grads[layer] = (
            head_block(summed_quarter(qkv_grad), 3),
            head_block(summed_quarter(out_grad), 1)[:, 0],
            ff_block(summed_quarter(fc_grad)),
            ff_block(summed_quarter(proj_grad)),
        )
        vector_grads[layer] = (
            jnp.stack([more_sums[0], sums[1], more_sums[1], sums[2], sums[3], sums[0]]),
            jnp.sum(rows(grad_qkv).astype(f32), 0).reshape(3, WIN),
            jnp.sum(rows(grad_pre).astype(f32), 0),
        )
    wide = lax.psum(jnp.stack([v[0] for v in vector_grads]), ("seq", "col", "row"))
    wide = lax.dynamic_slice_in_dim(wide, row * half_d, half_d, 2)
    slots = jnp.stack([v[1] for v in vector_grads])[:, 0::2]
    slots = jnp.where(kept, slots, jnp.zeros_like(slots))
    spread = jnp.zeros((layers, 2, D + HDIM), f32)
    spread = lax.dynamic_update_slice_in_dim(spread, slots, STEP * device, 2)[..., :D]
    qv_total = lax.psum(spread, ("seq", "col", "row"))
    qv_total = lax.dynamic_slice_in_dim(qv_total, col * 400, 400, 2)
    fc_total = lax.psum(jnp.stack([v[2] for v in vector_grads]), "seq")
    fc_total = lax.all_gather(fc_total, "row", axis=1, tiled=True)
    member = lambda index: jnp.stack([grads[layer][index] for layer in range(layers)]).astype(f32)
    return (
        own_columns(stream),
        own_columns(grad),
        wide[:, 0:2],
        wide[:, 2:4],
        member(0),
        qv_total,
        member(1),
        wide[:, 4:6],
        member(2),
        fc_total,
        member(3),
    )


def solution(mesh):
    in_specs = (
        P("row", ("seq", "col")),
        P("row", ("seq", "col")),
        P(None, None, "row"),
        P(None, None, "row"),
        P(None, "row", None, "col"),
        P(None, None, "col"),
        P(None, "row", "col"),
        P(None, None, "row"),
        P(None, "row", "col"),
        P(None, "col"),
        P(None, "row", "col"),
    )
    out_specs = (
        P("row", ("seq", "col")),
        P("row", ("seq", "col")),
        P(None, None, "row"),
        P(None, None, "row"),
        P(None, "row", None, "col"),
        P(None, None, "col"),
        P(None, "row", "col"),
        P(None, None, "row"),
        P(None, "row", "col"),
        P(None, "col"),
        P(None, "row", "col"),
    )
    fits = (mesh.shape["seq"], mesh.shape["row"], mesh.shape["col"]) == (4, 2, 4)
    return jax.shard_map(
        per_device_plane if fits else per_device_any, mesh=mesh, in_specs=in_specs, out_specs=out_specs, check_vma=False
    )
```

```python
import functools
import math

import jax
import jax.numpy as jnp
from jax import lax
from jax.experimental import pallas as pl
from jax.experimental.pallas import tpu as pltpu
from jax.sharding import PartitionSpec as P

HEADS = 25
HDIM = 64
D = 1600
SPAN = 256
SLOTS = 4
PLANE = ("col", "row")

norm_eps = 1e-05
bf16 = jnp.bfloat16
f32 = jnp.float32


def dot_nn(left, right):
    return lax.dot_general(left, right, (((1,), (0,)), ((), ())), preferred_element_type=f32)


def dot_nt(left, right):
    return lax.dot_general(left, right, (((1,), (1,)), ((), ())), preferred_element_type=f32)


def dot_tn(left, right):
    return lax.dot_general(left, right, (((0,), (0,)), ((), ())), preferred_element_type=f32)


def swap_rows(values, split, concat):
    return lax.all_to_all(values, "row", split_axis=split, concat_axis=concat, tiled=True)


def plane_gather(values):
    return lax.all_gather(values, PLANE, axis=0, tiled=True)


def plane_sum(partial):
    return lax.psum_scatter(partial.astype(bf16), PLANE, scatter_dimension=0, tiled=True).astype(f32)


def partner_swap(values):
    count = lax.axis_size("row")
    return lax.ppermute(values, "row", [(low, low ^ 1) for low in range(count)])


def rows_to_heads(values):
    rows, parts, width = values.shape
    slots = lax.axis_size("seq") * 2 * SLOTS * HDIM
    values = jnp.pad(values, ((0, 0), (0, 0), (0, slots - width)))
    values = lax.all_to_all(values, "seq", split_axis=2, concat_axis=0, tiled=True)
    side = lax.axis_index("row") % 2
    half = SLOTS * HDIM
    own = lax.dynamic_slice_in_dim(values, side * half, half, 2)
    other = partner_swap(lax.dynamic_slice_in_dim(values, (1 - side) * half, half, 2))
    low = jnp.where(side == 0, own, other).reshape(-1, 1, rows, parts, half)
    high = jnp.where(side == 0, other, own).reshape(-1, 1, rows, parts, half)
    return jnp.concatenate([low, high], 1).reshape(-1, parts, half)


def heads_to_rows(values):
    positions, parts, half = values.shape
    count = lax.axis_size("seq")
    rows = positions // (2 * count)
    values = values.reshape(count, 2, rows, parts, half)
    side = lax.axis_index("row") % 2
    own = jnp.where(side == 0, values[:, 0], values[:, 1]).reshape(count * rows, parts, half)
    given = jnp.where(side == 0, values[:, 1], values[:, 0]).reshape(count * rows, parts, half)
    other = partner_swap(given)
    both = jnp.concatenate(
        [jnp.where(side == 0, own, other), jnp.where(side == 0, other, own)], 2
    )
    both = lax.all_to_all(both, "seq", split_axis=0, concat_axis=2, tiled=True)
    return both[:, :, :D]


def cols_to_rows(values):
    return lax.all_to_all(values, PLANE, split_axis=0, concat_axis=2, tiled=True)


def rows_to_cols(values):
    return lax.all_to_all(values, PLANE, split_axis=2, concat_axis=0, tiled=True)


def sum_weights(grad, own_shape):
    rows, cols = lax.axis_size("row"), lax.axis_size("seq")
    width = grad.shape[-1]
    split = grad.astype(bf16).reshape(rows, cols, -1, width)
    split = lax.psum_scatter(split, "seq", scatter_dimension=1, tiled=True)[:, 0]
    split = lax.all_to_all(split, "row", split_axis=0, concat_axis=0, tiled=True)
    return lax.all_gather(split, "seq", axis=0, tiled=False)


def masked_scores(query, keys, block):
    scores = dot_nt(query, keys)
    rows, width = scores.shape
    row_at = lax.broadcasted_iota(jnp.int32, (rows, width), 0) + block * rows
    col_at = lax.broadcasted_iota(jnp.int32, (rows, width), 1)
    return jnp.where(col_at <= row_at, scores, -1e30)


def softmax_rows(scores):
    weights = jnp.exp(scores - jnp.max(scores, 1, keepdims=True))
    return weights * (1.0 / jnp.sum(weights, 1, keepdims=True))


def attend_kernel(q_ref, k_ref, v_ref, out_ref):
    blocks = q_ref.shape[0] // SPAN
    for block in range(blocks):
        rows = slice(block * SPAN, (block + 1) * SPAN)
        seen = slice(0, (block + 1) * SPAN)
        parts = []
        for head in range(2):
            cols = slice(head * HDIM, (head + 1) * HDIM)
            query = q_ref[rows, cols] * bf16(HDIM**-0.5)
            weights = softmax_rows(masked_scores(query, k_ref[seen, cols], block))
            parts.append(dot_nn(weights.astype(bf16), v_ref[seen, cols]))
        out_ref[rows, :] = jnp.concatenate(parts, 1).astype(bf16)


def attend_back_kernel(q_ref, k_ref, v_ref, da_ref, dq_ref, dk_ref, dv_ref, dk_sum, dv_sum):
    blocks = q_ref.shape[0] // SPAN
    dk_sum[...] = jnp.zeros_like(dk_sum)
    dv_sum[...] = jnp.zeros_like(dv_sum)
    for block in range(blocks):
        rows = slice(block * SPAN, (block + 1) * SPAN)
        seen = slice(0, (block + 1) * SPAN)
        dq_parts, dk_parts, dv_parts = [], [], []
        for head in range(2):
            cols = slice(head * HDIM, (head + 1) * HDIM)
            query = q_ref[rows, cols] * bf16(HDIM**-0.5)
            keys, grad = k_ref[seen, cols], da_ref[rows, cols]
            weights = softmax_rows(masked_scores(query, keys, block))
            grad_weights = dot_nt(grad, v_ref[seen, cols])
            along = jnp.sum(grad_weights * weights, 1, keepdims=True)
            grad_scores = (weights * (grad_weights - along)).astype(bf16)
            dq_parts.append(dot_nn(grad_scores, keys) * HDIM**-0.5)
            dk_parts.append(dot_tn(grad_scores, query))
            dv_parts.append(dot_tn(weights.astype(bf16), grad))
        dq_ref[rows, :] = jnp.concatenate(dq_parts, 1).astype(bf16)
        dk_sum[seen, :] += jnp.concatenate(dk_parts, 1)
        dv_sum[seen, :] += jnp.concatenate(dv_parts, 1)
    dk_ref[...] = dk_sum[...].astype(bf16)
    dv_ref[...] = dv_sum[...].astype(bf16)


def attend(qkv):
    positions = qkv.shape[0]
    pairs = SLOTS // 2
    flat = qkv.reshape(positions, 3 * SLOTS * HDIM)
    spec = lambda part: pl.BlockSpec((positions, 2 * HDIM), lambda i: (0, part * pairs + i))
    return pl.pallas_call(
        attend_kernel,
        grid=(pairs,),
        in_specs=[spec(0), spec(1), spec(2)],
        out_specs=spec(0),
        out_shape=jax.ShapeDtypeStruct((positions, SLOTS * HDIM), bf16),
        compiler_params=pltpu.CompilerParams(vmem_limit_bytes=48 << 20),
        name="attend",
    )(flat, flat, flat)


def attend_back(qkv, grad):
    positions = qkv.shape[0]
    pairs = SLOTS // 2
    flat = qkv.reshape(positions, 3 * SLOTS * HDIM)
    spec = lambda part: pl.BlockSpec((positions, 2 * HDIM), lambda i: (0, part * pairs + i))
    shape = jax.ShapeDtypeStruct((positions, SLOTS * HDIM), bf16)
    grads = pl.pallas_call(
        attend_back_kernel,
        grid=(pairs,),
        in_specs=[spec(0), spec(1), spec(2), spec(0)],
        out_specs=[spec(0)] * 3,
        out_shape=[shape] * 3,
        scratch_shapes=[pltpu.VMEM((positions, 2 * HDIM), f32)] * 2,
        compiler_params=pltpu.CompilerParams(vmem_limit_bytes=48 << 20),
        name="attend_back",
    )(flat, flat, flat, grad)
    return jnp.stack(grads, 1)


def norm_forward(stream, gain, shift):
    mean_value = jnp.mean(stream, 1, keepdims=True)
    centred = stream - mean_value
    inverse = lax.rsqrt(jnp.mean(centred * centred, 1, keepdims=True) + norm_eps)
    normal_part = centred * inverse
    return ((normal_part * gain + shift).astype(bf16), normal_part, inverse)


def norm_backward(grad_out, normal_part, inverse, gain):
    scaled = grad_out * gain
    grad_in = inverse * (
        scaled
        - jnp.mean(scaled, 1, keepdims=True)
        - normal_part * jnp.mean(scaled * normal_part, 1, keepdims=True)
    )
    return (grad_in, jnp.sum(grad_out * normal_part, 0), jnp.sum(grad_out, 0))


def activation(values):
    return jax.nn.gelu(values, approximate=True)


def activation_grad(values, grad_values):
    unused_value, pullback = jax.vjp(activation, values)
    return pullback(grad_values)[0]


def per_device_any(
    tokens, cotangent, norm_gain, norm_bias, w_qkv, b_qv, w_out, out_bias, w_fc, b_fc, w_proj
):
    layers = w_qkv.shape[0]
    row_width = tokens.shape[0]
    col_width = w_out.shape[2]
    ff_width = w_fc.shape[2]
    n_rows, row = lax.axis_size("row"), lax.axis_index("row")
    own_cols, own_ff = col_width // n_rows, ff_width // n_rows

    vectors = jnp.stack([norm_gain, norm_bias, out_bias])
    vectors = lax.all_gather(vectors, "row", axis=3, tiled=True)
    gains, shifts, out_shifts = vectors[0], vectors[1], vectors[2]
    qv_bias = lax.dynamic_slice_in_dim(b_qv, row * own_cols, own_cols, 2)
    fc_bias = lax.dynamic_slice_in_dim(b_fc, row * own_ff, own_ff, 1)

    stream = swap_rows(tokens, 1, 0).T
    weights = []
    for layer in range(layers):
        qkv_matrix = swap_rows(w_qkv[layer].astype(bf16), 2, 0).reshape(D, 3 * own_cols)
        out_matrix = lax.all_gather(w_out[layer].astype(bf16), "row", axis=0, tiled=True)
        out_matrix = lax.all_gather(out_matrix, "col", axis=1, tiled=True)
        fc_matrix = swap_rows(w_fc[layer].astype(bf16), 1, 0)
        proj_matrix = swap_rows(w_proj[layer].astype(bf16), 1, 0)
        weights.append((qkv_matrix, out_matrix, fc_matrix, proj_matrix))
    saved = []
    for layer in range(layers):
        qkv_matrix, out_matrix, fc_matrix, proj_matrix = weights[layer]
        normed, normal_one, inverse_one = norm_forward(stream, gains[layer, 0], shifts[layer, 0])
        all_one = plane_gather(normed)
        bias = jnp.concatenate(
            [qv_bias[layer, 0], jnp.zeros_like(qv_bias[layer, 0]), qv_bias[layer, 1]]
        )
        qkv_cols = (dot_nn(all_one, qkv_matrix) + bias).astype(bf16)
        qkv = rows_to_heads(cols_to_rows(qkv_cols.reshape(-1, 3, own_cols)))
        attended = heads_to_rows(attend(qkv)[:, None])
        att_cols = rows_to_cols(attended)[:, 0]
        attended = attended[:, 0]
        residual = stream + (dot_nt(attended, out_matrix) + out_shifts[layer, 0])
        normed, normal_two, inverse_two = norm_forward(residual, gains[layer, 1], shifts[layer, 1])
        all_two = plane_gather(normed)
        pre_act = dot_nn(all_two, fc_matrix) + fc_bias[layer]
        act = activation(pre_act).astype(bf16)
        stream = residual + (plane_sum(dot_nt(act, proj_matrix)) + out_shifts[layer, 1])
        saved.append(
            (all_one, normal_one, inverse_one, qkv, att_cols, all_two, normal_two, inverse_two, pre_act, act)
        )
    grad_stream = swap_rows(cotangent, 1, 0).T
    grads = [None] * layers
    vector_grads = [None] * layers
    for layer in reversed(range(layers)):
        qkv_matrix, out_matrix, fc_matrix, proj_matrix = weights[layer]
        all_one, normal_one, inverse_one, qkv, att_cols, all_two, normal_two, inverse_two, pre_act, act = saved[layer]
        grad_low = grad_stream.astype(bf16)
        proj_shift = jnp.sum(grad_low.astype(f32), 0)
        all_grad = plane_gather(grad_low)
        proj_grad = sum_weights(dot_tn(all_grad, act), w_proj.shape[1:])
        grad_pre = activation_grad(pre_act, dot_nn(all_grad, proj_matrix)).astype(bf16)
        fc_grad = sum_weights(dot_tn(all_two, grad_pre), w_fc.shape[1:])
        fc_shift = jnp.sum(grad_pre.astype(f32), 0)
        grad_normed = plane_sum(dot_nt(grad_pre, fc_matrix))
        grad_in, gain_two, shift_two = norm_backward(grad_normed, normal_two, inverse_two, gains[layer, 1])
        grad_res = grad_stream + grad_in
        grad_low = grad_res.astype(bf16)
        out_shift = jnp.sum(grad_low.astype(f32), 0)
        grad_att = dot_nn(grad_low, out_matrix).astype(bf16)
        out_grad = sum_weights(dot_tn(plane_gather(grad_low), att_cols), w_out.shape[1:])
        grad_heads = rows_to_heads(grad_att[:, None])[:, 0]
        grad_rows = heads_to_rows(attend_back(qkv, grad_heads))
        grad_cols = rows_to_cols(grad_rows).reshape(-1, 3 * own_cols)
        qkv_grad = sum_weights(dot_tn(all_one, grad_cols), w_qkv.shape[1:])
        bias_sums = jnp.sum(grad_cols.astype(f32), 0).reshape(3, own_cols)
        grad_normed = plane_sum(dot_nt(grad_cols, qkv_matrix))
        grad_in, gain_one, shift_one = norm_backward(grad_normed, normal_one, inverse_one, gains[layer, 0])
        grad_stream = grad_res + grad_in
        grads[layer] = (qkv_grad, out_grad, fc_grad, proj_grad)
        vector_grads[layer] = (
            jnp.stack([jnp.stack([gain_one, gain_two]), jnp.stack([shift_one, shift_two]), jnp.stack([out_shift, proj_shift])]),
            jnp.stack([bias_sums[0], bias_sums[2]]),
            fc_shift,
        )
    wide = lax.psum(jnp.stack([v[0] for v in vector_grads]), ("seq", "col", "row"))
    wide = lax.dynamic_slice_in_dim(wide, row * row_width, row_width, 3)
    slim = jnp.concatenate(
        [jnp.concatenate([v[1].reshape(2, own_cols), v[2].reshape(ff_width // col_width, own_cols)]) for v in vector_grads]
    ).reshape(layers, -1, own_cols)
    slim_qv = lax.psum(jnp.stack([v[1] for v in vector_grads]), "seq")
    slim_fc = lax.psum(jnp.stack([v[2] for v in vector_grads]), "seq")
    qv_total = lax.all_gather(slim_qv, "row", axis=2, tiled=True)
    fc_total = lax.all_gather(slim_fc, "row", axis=1, tiled=True)

    def as_grid(member, shape):
        done = []
        for layer in range(layers):
            blocks = grads[layer][member]
            n_seq, parts = blocks.shape[:2]
            if len(shape) == 3:
                blocks = blocks.reshape(n_seq, parts, -1, 3, own_cols).transpose(0, 2, 3, 1, 4)
            else:
                blocks = blocks.transpose(0, 2, 1, 3)
            done.append(blocks.reshape(shape).astype(f32))
        return jnp.stack(done)

    return (
        swap_rows(stream.T, 0, 1),
        swap_rows(grad_stream.T, 0, 1),
        wide[:, 0],
        wide[:, 1],
        as_grid(0, w_qkv.shape[1:]),
        qv_total,
        as_grid(1, w_out.shape[1:]),
        wide[:, 2],
        as_grid(2, w_fc.shape[1:]),
        fc_total,
        as_grid(3, w_proj.shape[1:]),
    )


MESH = pl.DeviceIdType.MESH
DMA = pltpu.SemaphoreType.DMA
BLOCK = 128
WIN = SLOTS * HDIM
VMEM = pltpu.VMEM
STEP = 3 * HDIM


def place():
    col, row = lax.axis_index("col"), lax.axis_index("row")
    flip = col + 1 - 2 * lax.rem(col, 2)
    far = lax.rem(col + 2, 4)
    cross = lax.rem(flip + 2, 4)
    return col, flip, far, cross, row, 1 - row


def greet(along_seq):
    col, flip, far, cross, row, other = place()
    barrier = pltpu.get_barrier_semaphore()
    partners = [{"col": flip}, {"row": other}, {"col": far}]
    if along_seq:
        here = lax.axis_index("seq")
        partners += [{"seq": lax.rem(here + step, 4)} for step in (1, 2, 3)]
    for partner in partners:
        pl.semaphore_signal(barrier, inc=1, device_id=partner, device_id_type=MESH)
    pl.semaphore_wait(barrier, len(partners))


def remote(src, dst, send, recv, index, device):
    return pltpu.make_async_remote_copy(
        src_ref=src,
        dst_ref=dst,
        send_sem=send.at[index],
        recv_sem=recv.at[index],
        device_id=device,
        device_id_type=MESH,
    )


GATHER_SCRATCH = [DMA((10,)), DMA((10,))]


def gather(full, send, recv, body):
    col, flip, far, cross, row, other = place()
    half = BLOCK // 2
    low, high = pl.ds(0, half), pl.ds(half, half)
    core, along_x, along_y = {"col": flip}, {"row": other}, {"col": far}

    def copy(index, ref, device):
        return remote(ref, ref, send, recv, index, device)

    copies = [
        copy(0, full.at[col, row], core),
        copy(1, full.at[col, row, low], along_x),
        copy(2, full.at[col, row, high], along_y),
        copy(3, full.at[col, row, high], along_x),
        copy(4, full.at[col, row, low], along_y),
        copy(5, full.at[col, other, low], along_y),
        copy(6, full.at[far, row, high], along_x),
        copy(7, full.at[col, other], core),
        copy(8, full.at[far, row], core),
        copy(9, full.at[far, other], core),
    ]
    for index in (1, 2, 0, 3, 4):
        copies[index].start()
    for arrived, started in ((1, 5), (2, 6), (3, 7), (4, 8)):
        copies[arrived].wait_recv()
        copies[started].start()
    body(col)
    copies[5].wait_recv()
    copies[6].wait_recv()
    copies[9].start()
    copies[0].wait_recv()
    copies[7].wait_recv()
    body(flip)
    body(far)
    copies[8].wait_recv()
    copies[9].wait_recv()
    body(cross)
    for each in copies:
        each.wait_send()


SCATTER_SCRATCH = [
    VMEM((2, 2, BLOCK, D), bf16),
    VMEM((2, 2, BLOCK, D), bf16),
    VMEM((2, 2, BLOCK, D), bf16),
    VMEM((2, BLOCK, D), f32),
    VMEM((3, BLOCK // 2, D), bf16),
    VMEM((3, BLOCK // 2, D), bf16),
    VMEM((2, BLOCK // 2, D), bf16),
    DMA((8,)),
    DMA((8,)),
]


def scatter(compute, given, taken, part, own, from_x, from_y, turn, send, recv):
    col, flip, far, cross, row, other = place()
    half = BLOCK // 2
    low, high = pl.ds(0, half), pl.ds(half, half)
    core, along_x, along_y = {"col": flip}, {"row": other}, {"col": far}

    def copy(index, src, dst, device):
        return remote(src, dst, send, recv, index, device)

    sib_own = copy(0, given.at[1], taken.at[1], core)
    sib_far = copy(1, given.at[0], taken.at[0], core)
    x_far = copy(2, part.at[0, other, low], from_x.at[1], along_x)
    y_far = copy(3, part.at[0, other, high], from_y.at[1], along_y)
    y_own = copy(4, part.at[0, row, high], from_y.at[0], along_y)
    x_own = copy(5, part.at[1, other, low], from_x.at[0], along_x)
    y_turn = copy(6, turn.at[0], from_y.at[2], along_y)
    x_turn = copy(7, turn.at[1], from_x.at[2], along_x)
    shape = (2, BLOCK, D)
    given[1] = compute(flip).reshape(shape).astype(bf16)
    sib_own.start()
    given[0] = compute(cross).reshape(shape).astype(bf16)
    sib_far.start()
    value = compute(far).reshape(shape)
    sib_far.wait_recv()
    part[0] = (value + taken[0].astype(f32)).astype(bf16)
    x_far.start()
    y_far.start()
    y_own.start()
    value = compute(col).reshape(shape)
    sib_own.wait_recv()
    own[...] = value + taken[1].astype(f32)
    part[1] = own[...].astype(bf16)
    x_own.start()
    x_far.wait_recv()
    turn[0] = (part[0, row, low].astype(f32) + from_x[1].astype(f32)).astype(bf16)
    y_turn.start()
    y_far.wait_recv()
    turn[1] = (own[other, high] + from_y[1].astype(f32)).astype(bf16)
    x_turn.start()
    x_own.wait_recv()
    y_own.wait_recv()
    y_turn.wait_recv()
    x_turn.wait_recv()
    total = jnp.concatenate(
        [
            own[row, low] + from_x[0].astype(f32) + from_y[2].astype(f32),
            own[row, high] + from_y[0].astype(f32) + from_x[2].astype(f32),
        ],
        0,
    )
    for each in (sib_own, sib_far, x_far, y_far, y_own, x_own, y_turn, x_turn):
        each.wait_send()
    return total


SEQ_SCRATCH = [DMA((4,)), DMA((4,))]


def seq_copy(src, dst, send, recv, group):
    here = lax.axis_index("seq")
    return pltpu.make_async_remote_copy(
        src_ref=src.at[group],
        dst_ref=dst.at[here],
        send_sem=send.at[group],
        recv_sem=recv.at[here],
        device_id={"seq": group},
        device_id_type=MESH,
    )


def seq_send(src, dst, send, recv, group):
    here = lax.axis_index("seq")

    @pl.when(group != here)
    def _():
        seq_copy(src, dst, send, recv, group).start()

    @pl.when(group == here)
    def _():
        dst[here] = src[here]


def seq_wait(src, dst, send, recv, group):
    @pl.when(group != lax.axis_index("seq"))
    def _():
        pltpu.make_async_remote_copy(
            src_ref=src.at[group],
            dst_ref=dst.at[group],
            send_sem=send.at[group],
            recv_sem=recv.at[group],
            device_id={"seq": group},
            device_id_type=MESH,
        ).wait_recv()


def seq_sent(src, dst, send, recv):
    for group in range(4):

        @pl.when(group != lax.axis_index("seq"))
        def _():
            seq_copy(src, dst, send, recv, group).wait_send()


class Matrix:
    def __init__(self, own, came, target, sems):
        row = lax.axis_index("row")
        self.target = target
        self.copies = [
            pltpu.make_async_copy(own, target.at[row], sems.at[0]),
            pltpu.make_async_copy(came, target.at[1 - row], sems.at[1]),
        ]

    def start(self):
        for each in self.copies:
            each.start()

    def wait(self):
        for each in self.copies:
            each.wait()

    def rows(self):
        return self.target[...].reshape(D, -1)

    def halves(self):
        return self.target[0], self.target[1]


def by_features(values, halves):
    half = D // 2
    return dot_nt(values[:, :half], halves[0]) + dot_nt(values[:, half:], halves[1])


def to_features(values, halves):
    return jnp.concatenate([dot_nn(values, halves[0]), dot_nn(values, halves[1])], 1)


PIECE = 160


def swap_scratch(arrays, pieces):
    return [DMA((arrays * pieces,)), DMA((arrays * pieces,))]


class Swaps:
    def __init__(self, pairs, send, recv):
        self.pieces, self.begun = [], 0
        for given, out in pairs:
            height = given.shape[0]
            for low in range(0, height, PIECE):
                rows = pl.ds(low, min(PIECE, height - low))
                self.pieces.append(
                    remote(given.at[rows], out.at[rows], send, recv, len(self.pieces), {"row": 1 - lax.axis_index("row")})
                )

    def start(self, count):
        for each in self.pieces[self.begun : self.begun + count]:
            each.start()
        self.begun = min(self.begun + count, len(self.pieces))

    def finish(self):
        self.start(len(self.pieces))
        for each in self.pieces:
            each.wait()


QUARTER = 192


def spread_scratch(arrays):
    return [DMA((2, arrays))] * 2 + [DMA((arrays, 4))] * 2


class Spread:
    def __init__(self, pairs, x_send, x_recv, z_send, z_recv):
        row, here = lax.axis_index("row"), lax.axis_index("seq")
        quarter = pl.ds(pl.multiple_of(here * QUARTER, 16), QUARTER)
        rest = pl.ds(4 * QUARTER, 32)
        self.swaps, self.sends, self.waits = [], [], []
        for index, (given, out) in enumerate(pairs):
            for kind, rows in enumerate((quarter, rest)):
                self.swaps.append(
                    remote(given.at[rows], out.at[rows], x_send.at[kind], x_recv.at[kind], index, {"row": 1 - row})
                )
            came = out.at[quarter]
            for step in (1, 2, 3):
                to = lax.rem(here + step, 4)
                self.sends.append(
                    pltpu.make_async_remote_copy(
                        src_ref=came, dst_ref=came, send_sem=z_send.at[index, to],
                        recv_sem=z_recv.at[index, here], device_id={"seq": to}, device_id_type=MESH,
                    )
                )
                theirs = out.at[pl.ds(pl.multiple_of(to * QUARTER, 16), QUARTER)]
                self.waits.append(
                    pltpu.make_async_remote_copy(
                        src_ref=theirs, dst_ref=theirs, send_sem=z_send.at[index, to],
                        recv_sem=z_recv.at[index, to], device_id={"seq": to}, device_id_type=MESH,
                    )
                )

    def start(self):
        for each in self.swaps:
            each.start()

    def forward(self):
        for each in self.swaps:
            each.wait_recv()
        for each in self.sends:
            each.start()

    def finish(self):
        for each in self.waits:
            each.wait_recv()
        for each in self.sends + self.swaps:
            each.wait_send()


def norm_rows(stream):
    mean_value = jnp.mean(stream, 1, keepdims=True)
    centred = stream - mean_value
    inverse = lax.rsqrt(jnp.mean(centred * centred, 1, keepdims=True) + norm_eps)
    return centred * inverse, inverse


def attention_forward(
    stream, gain, shift, w_own, w_came, bias, given_0, given_1,
    full, heads, att, out_0, out_1,
    w, qkv, sent, w_sem, g_send, g_recv, q_send, q_recv, a_send, a_recv, *swap_sems,
):
    moves = Swaps(((given_1, out_1), (given_0, out_0)), *swap_sems)
    col, flip, far, cross, row, other = place()
    weights = Matrix(w_own, w_came, w, w_sem)
    weights.start()
    greet(True)
    normal_part, unused = norm_rows(stream[...])
    full[col, row] = (normal_part * gain[...] + shift[...]).astype(bf16)
    seen = []

    def project(group):
        if not seen:
            weights.wait()
        seen.append(0)
        rows = full[group].reshape(2 * BLOCK, D)
        qkv[group] = (by_features(rows, weights.halves()) + bias[...]).astype(bf16)
        seq_send(qkv, heads, q_send, q_recv, group)

    gather(full, g_send, g_recv, project)
    moves.start(2)
    for block in range(4):
        seq_wait(qkv, heads, q_send, q_recv, block)
        keys_seen = (block + 1) * SPAN
        for pair in range(SLOTS // 2):
            parts = []
            for head in range(2):
                low = (2 * pair + head) * HDIM
                query = heads[block, :, low : low + HDIM] * bf16(HDIM**-0.5)
                keys = heads[: block + 1, :, WIN + low : WIN + low + HDIM].reshape(keys_seen, HDIM)
                values = heads[: block + 1, :, 2 * WIN + low : 2 * WIN + low + HDIM].reshape(keys_seen, HDIM)
                p = softmax_rows(masked_scores(query, keys, block)).astype(bf16)
                parts.append(dot_nn(p, values))
            sent[block, :, 2 * pair * HDIM : 2 * (pair + 1) * HDIM] = jnp.concatenate(parts, 1).astype(bf16)
            moves.start(1)
        seq_send(sent, att, a_send, a_recv, block)
    for block in range(4):
        seq_wait(sent, att, a_send, a_recv, block)
    seq_sent(qkv, heads, q_send, q_recv)
    seq_sent(sent, att, a_send, a_recv)
    moves.finish()


def gelu_terms(values):
    k = math.sqrt(2 / math.pi)
    squares = values * values
    t = jnp.tanh(values * (k + (k * 0.044715) * squares))
    return t, squares


def masked_out(matrix):
    col, flip, far, cross, row, other = place()
    kept = jnp.where(2 * col + row == 7, WIN, STEP)
    height = lax.broadcasted_iota(jnp.int32, (WIN, 1), 0)
    return [jnp.where(height < kept, half, jnp.zeros_like(half)) for half in matrix.halves()]


def mlp_forward(last, *refs):
    (att, stream, out_own, out_came, out_shift, gain, shift, fc_own, fc_came, fc_bias, proj_shift,
     proj_own, proj_came, given_0,
     res, full, pre, act, result, out_0,
     w_out, fc, proj, w_sem, g_send, g_recv, *scratch) = refs
    if last:
        moves = Swaps(((given_0, out_0),), *scratch[:2])
        scratch = scratch[2:]
    else:
        spread = Spread(((given_0, out_0),), *scratch[:4])
        scratch = scratch[4:]
    col, flip, far, cross, row, other = place()
    out_matrix = Matrix(out_own, out_came, w_out, w_sem.at[0])
    fc_matrix = Matrix(fc_own, fc_came, fc, w_sem.at[1])
    proj_matrix = Matrix(proj_own, proj_came, proj, w_sem.at[2])
    out_matrix.start()
    fc_matrix.start()
    proj_matrix.start()
    greet(not last)
    out_matrix.wait()
    count = len(SCATTER_SCRATCH)
    w_out_rows = masked_out(out_matrix)
    if not last:
        spread.start()

    def out_terms(group):
        if last:
            moves.start(1)
        return to_features(att[group], w_out_rows)

    total = scatter(out_terms, *scratch[:count])
    res[...] = stream[...] + (total + out_shift[...])
    normal_part, unused = norm_rows(res[...])
    full[col, row] = (normal_part * gain[...] + shift[...]).astype(bf16)
    if not last:
        spread.forward()
    seen = []

    def widen(group):
        if not seen:
            fc_matrix.wait()
        seen.append(0)
        u = dot_nn(full[group].reshape(2 * BLOCK, D), fc_matrix.rows()) + fc_bias[...]
        pre[group] = u
        t, unused = gelu_terms(u)
        act[group] = (0.5 * u * (1 + t)).astype(bf16)

    gather(full, g_send, g_recv, widen)
    if last:
        moves.finish()
    proj_matrix.wait()
    total = scatter(lambda group: dot_nt(act[group], proj_matrix.rows()), *scratch[count:])
    result[...] = res[...] + (total + proj_shift[...])
    if not last:
        spread.finish()


def norm_back_rows(grad_out, normal_part, inverse, gain):
    scaled = grad_out * gain
    return inverse * (
        scaled
        - jnp.mean(scaled, 1, keepdims=True)
        - normal_part * jnp.mean(scaled * normal_part, 1, keepdims=True)
    )


def mlp_backward(
    grad, res, gain, pre_hbm, fc_own, fc_came, proj_own, proj_came, out_own, out_came,
    full, grad_pre, full_res, grad_res, grad_att, sums,
    w_out, fc, proj, pre, w_sem, g_send, g_recv, h_send, h_recv, *scratch,
):
    col, flip, far, cross, row, other = place()
    out_matrix = Matrix(out_own, out_came, w_out, w_sem.at[0])
    fc_matrix = Matrix(fc_own, fc_came, fc, w_sem.at[1])
    proj_matrix = Matrix(proj_own, proj_came, proj, w_sem.at[2])
    pre_copy = pltpu.make_async_copy(pre_hbm, pre, w_sem.at[3, 0])
    proj_matrix.start()
    pre_copy.start()
    fc_matrix.start()
    out_matrix.start()
    greet(False)
    low = grad[...].astype(bf16)
    full[col, row] = low
    sums[0:1, :] = jnp.sum(low.astype(f32), 0, keepdims=True)
    seen = []

    def widen(group):
        if not seen:
            proj_matrix.wait()
            pre_copy.wait()
        seen.append(0)
        grad_act = dot_nn(full[group].reshape(2 * BLOCK, D), proj_matrix.rows())
        u = pre[group]
        t, squares = gelu_terms(u)
        k = math.sqrt(2 / math.pi)
        slope = 0.5 * (1 + t) + 0.5 * u * (1 - t * t) * (k + (3 * k * 0.044715) * squares)
        grad_pre[group] = (grad_act * slope).astype(bf16)

    gather(full, g_send, g_recv, widen)
    fc_matrix.wait()
    total = scatter(lambda group: dot_nt(grad_pre[group], fc_matrix.rows()), *scratch)
    normal_part, inverse = norm_rows(res[...])
    sums[1:2, :] = jnp.sum(total * normal_part, 0, keepdims=True)
    sums[2:3, :] = jnp.sum(total, 0, keepdims=True)
    grad_res[...] = grad[...] + norm_back_rows(total, normal_part, inverse, gain[...])
    low = grad_res[...].astype(bf16)
    full_res[col, row] = low
    sums[3:4, :] = jnp.sum(low.astype(f32), 0, keepdims=True)
    sums[4:8, :] = jnp.zeros((4, D), f32)

    out_matrix.wait()
    w_out_rows = masked_out(out_matrix)

    def out_back(group):
        grad_att[group] = by_features(full_res[group].reshape(2 * BLOCK, D), w_out_rows).astype(bf16)

    gather(full_res, h_send, h_recv, out_back)


def attention_backward(
    heads, grad_att, grad_res, stream, gain, w_own, w_came,
    grad_qkv, result, sums,
    w, da, dk, dv, sent, w_sem, a_send, a_recv, q_send, q_recv, *scratch,
):
    weights = Matrix(w_own, w_came, w, w_sem)
    weights.start()
    greet(True)
    for group in range(4):
        seq_send(grad_att, da, a_send, a_recv, group)
    for block in (3, 2, 1, 0):
        seq_wait(grad_att, da, a_send, a_recv, block)
        keys_seen = (block + 1) * SPAN
        for pair in range(SLOTS // 2):
            dq_parts, dk_parts, dv_parts = [], [], []
            for head in range(2):
                low = (2 * pair + head) * HDIM
                query = heads[block, :, low : low + HDIM] * bf16(HDIM**-0.5)
                keys = heads[: block + 1, :, WIN + low : WIN + low + HDIM].reshape(keys_seen, HDIM)
                values = heads[: block + 1, :, 2 * WIN + low : 2 * WIN + low + HDIM].reshape(keys_seen, HDIM)
                grad = da[block, :, low : low + HDIM]
                p = softmax_rows(masked_scores(query, keys, block))
                dp = dot_nt(grad, values)
                ds = (p * (dp - jnp.sum(dp * p, 1, keepdims=True))).astype(bf16)
                dq_parts.append(dot_nn(ds, keys) * HDIM**-0.5)
                dk_parts.append(dot_tn(ds, query))
                dv_parts.append(dot_tn(p.astype(bf16), grad))
            cols = slice(2 * pair * HDIM, 2 * (pair + 1) * HDIM)
            new_dk = jnp.concatenate(dk_parts, 1).reshape(block + 1, SPAN, 2 * HDIM)
            new_dv = jnp.concatenate(dv_parts, 1).reshape(block + 1, SPAN, 2 * HDIM)
            if block < 3:
                new_dk = new_dk + dk[: block + 1, :, cols]
                new_dv = new_dv + dv[: block + 1, :, cols]
            dk[: block + 1, :, cols] = new_dk
            dv[: block + 1, :, cols] = new_dv
            sent[block, :, cols] = jnp.concatenate(dq_parts, 1).astype(bf16)
        sent[block, :, WIN : 2 * WIN] = dk[block].astype(bf16)
        sent[block, :, 2 * WIN :] = dv[block].astype(bf16)
        seq_send(sent, grad_qkv, q_send, q_recv, block)
    weights.wait()
    for block in range(4):
        seq_wait(sent, grad_qkv, q_send, q_recv, block)
    total = scatter(lambda group: to_features(grad_qkv[group], weights.halves()), *scratch)
    normal_part, inverse = norm_rows(stream[...])
    sums[0:1, :] = jnp.sum(total * normal_part, 0, keepdims=True)
    sums[1:2, :] = jnp.sum(total, 0, keepdims=True)
    sums[2:8, :] = jnp.zeros((6, D), f32)
    result[...] = grad_res[...] + norm_back_rows(total, normal_part, inverse, gain[...])
    seq_sent(grad_att, da, a_send, a_recv)
    seq_sent(sent, grad_qkv, q_send, q_recv)


def call(kernel, ident, places, out_places, outs, scratch, cost, *operands):
    spaces = {"v": VMEM, "h": pl.ANY}
    return pl.pallas_call(
        kernel,
        in_specs=[pl.BlockSpec(memory_space=spaces[each]) for each in places],
        out_specs=[pl.BlockSpec(memory_space=spaces[each]) for each in out_places],
        out_shape=[jax.ShapeDtypeStruct(shape, kind) for shape, kind in outs],
        scratch_shapes=scratch,
        compiler_params=pltpu.CompilerParams(
            collective_id=ident, has_side_effects=True, vmem_limit_bytes=60 << 20
        ),
        cost_estimate=pl.CostEstimate(flops=cost, bytes_accessed=0, transcendentals=0),
        name=getattr(kernel, "func", kernel).__name__,
    )(*operands)


def partner_halves(own, given, axis):
    row = lax.axis_index("row")
    other = partner_swap(given)
    return jnp.concatenate(
        [jnp.where(row == 0, own, other), jnp.where(row == 0, other, own)], axis
    )


def ff_part(block, side):
    axis = block.ndim - 1
    full, wide = block.shape[axis] // 2, WIDE
    thin = full - wide
    return jnp.concatenate(
        [
            lax.dynamic_slice_in_dim(block, side * wide, wide, axis),
            lax.dynamic_slice_in_dim(block, 2 * wide + side * thin, thin, axis),
        ],
        axis,
    )


def ff_parts(block):
    row = lax.axis_index("row")
    return ff_part(block, row), ff_part(block, 1 - row)


def head_window(block, axis):
    col = lax.axis_index("col")
    edge = 3 * 16
    last = lax.slice_in_dim(block, block.shape[axis] - edge, block.shape[axis], axis=axis)
    left = lax.ppermute(last, "col", [(0, 1), (1, 2), (2, 3)])
    wide = jnp.concatenate([left, block, jnp.zeros_like(last)], axis)
    return lax.dynamic_slice_in_dim(wide, edge - 16 * col, 2 * STEP + HDIM, axis)


def head_parts(block):
    row = lax.axis_index("row")
    wide = head_window(block, 1)
    parts = [lax.dynamic_slice_in_dim(wide, side * STEP, WIN, 1) for side in (row, 1 - row)]
    return tuple(part.reshape(-1, part.shape[2]) for part in parts)


UNIT = 128
WIDE = 6 * UNIT
UNITS = 20
THIN = 32
COLS = 400
SLOTS_DEEP = 6
OWN_DEEP = 5
PART = 208
LAST = 3


def part_start(part):
    return pl.multiple_of(200 * part - 8 * lax.rem(part, 2), 16)


def sum_gradients(*refs):
    n_in = 16
    operands, small = refs[:n_in], refs[n_in]
    fc_out, proj_out, heads_out, small_out = refs[n_in + 1 : n_in + 5]
    (left_rows, right_cols_qkv, right_cols_att, right_cols_pre, right_cols_act, own, up, down, acc, fin, load,
     tails, out, done, done_tail, done_sem, wide, wide_sem, frag_send, frag_recv,
     up_send, up_recv, down_send, down_recv, swap_send, swap_recv, out_up_send, out_up_recv,
     out_down_send, out_down_recv, stage, inbox, line, s_send, s_recv, l_send, l_recv) = refs[n_in + 5 :]
    here, row = lax.axis_index("seq"), lax.axis_index("row")
    total = 2 * UNITS + 1
    last = LAST

    barrier = pltpu.get_barrier_semaphore()
    col, flip, far, cross, row, other = place()
    near = [{"col": flip}, {"row": other}, {"col": far}]
    partners = [{"row": other}] + [{axis: lax.rem(index + step, 4)} for axis, index in (("col", col), ("seq", here)) for step in (1, 2, 3)]
    for partner in partners:
        pl.semaphore_signal(barrier, inc=1, device_id=partner, device_id_type=MESH)
    pl.semaphore_wait(barrier, len(partners))

    def small_copy(hop):
        return remote(stage.at[hop], inbox.at[hop], s_send, s_recv, hop, near[hop])

    def line_copy(step):
        to = lax.rem(here + step, 4)
        return pltpu.make_async_remote_copy(
            src_ref=line.at[here], dst_ref=line.at[here], send_sem=l_send.at[to],
            recv_sem=l_recv.at[here], device_id={"seq": to}, device_id_type=MESH,
        )

    def line_wait(step):
        start = lax.rem(here + step, 4)
        pltpu.make_async_remote_copy(
            src_ref=line.at[start], dst_ref=line.at[start], send_sem=l_send.at[start],
            recv_sem=l_recv.at[start], device_id={"seq": start}, device_id_type=MESH,
        ).wait_recv()

    def small_step(hop):
        if hop == 0:
            stage[0] = small[...]
            small_copy(0).start()
        elif hop < 3:
            small_copy(hop - 1).wait()
            stage[hop] = stage[hop - 1] + inbox[hop - 1]
            small_copy(hop).start()
        elif hop == 3:
            small_copy(2).wait()
            line[here] = stage[2] + inbox[2]
            for step in (1, 2, 3):
                line_copy(step).start()
        else:
            for step in (1, 2, 3):
                line_wait(step)
                line_copy(step).wait_send()
            small_out[...] = (line[0] + line[1]) + (line[2] + line[3])

    def load_pair(layer, rows, cols_index, cols):
        pair = [
            pltpu.make_async_copy(operands[8 * layer + rows], left_rows, load.at[0]),
            pltpu.make_async_copy(operands[8 * layer + 4 + cols_index], cols, load.at[1]),
        ]
        for each in pair:
            each.start()
        for each in pair:
            each.wait()

    def slot_of(unit):
        return lax.rem(unit, SLOTS_DEEP)

    def own_slot(unit):
        return lax.rem(unit, OWN_DEEP)

    def own_part(unit, part):
        return own.at[own_slot(unit), :, pl.ds(part_start(part), PART)]

    def to_up(unit, part, src):
        slot = slot_of(unit)
        return pltpu.make_async_remote_copy(
            src_ref=src, dst_ref=up.at[slot, part], send_sem=up_send.at[slot, part],
            recv_sem=up_recv.at[slot, part], device_id={"seq": here + 1}, device_id_type=MESH,
        )

    def to_down(unit, part, src):
        slot = slot_of(unit)
        return pltpu.make_async_remote_copy(
            src_ref=src, dst_ref=down.at[slot, part], send_sem=down_send.at[slot, part],
            recv_sem=down_recv.at[slot, part], device_id={"seq": here - 1}, device_id_type=MESH,
        )

    def pass_up(unit, part):
        slot = slot_of(unit)
        to_up(unit, part, up.at[slot, part]).wait_recv()
        add = own[own_slot(unit), :, pl.ds(part_start(part), PART)].astype(f32)
        up[slot, part] = (up[slot, part].astype(f32) + add).astype(bf16)
        to_up(unit, part, up.at[slot, part]).start()

    def pass_down(unit, part):
        slot = slot_of(unit)
        to_down(unit, part, down.at[slot, part]).wait_recv()
        add = own[own_slot(unit), :, pl.ds(part_start(part), PART)].astype(f32)
        down[slot, part] = (down[slot, part].astype(f32) + add).astype(bf16)
        to_down(unit, part, down.at[slot, part]).start()

    def swap(unit):
        slot = slot_of(unit)
        return remote(
            fin.at[lax.rem(unit, 2)], out.at[slot, here, row], swap_send, swap_recv, slot, {"row": 1 - row}
        )

    def out_up(unit, part):
        slot = slot_of(unit)
        ref = out.at[slot, part]
        return pltpu.make_async_remote_copy(
            src_ref=ref, dst_ref=ref, send_sem=out_up_send.at[slot, part],
            recv_sem=out_up_recv.at[slot, part], device_id={"seq": here + 1}, device_id_type=MESH,
        )

    def out_down(unit, part):
        slot = slot_of(unit)
        ref = out.at[slot, part]
        return pltpu.make_async_remote_copy(
            src_ref=ref, dst_ref=ref, send_sem=out_down_send.at[slot, part],
            recv_sem=out_down_recv.at[slot, part], device_id={"seq": here - 1}, device_id_type=MESH,
        )

    def start(unit):
        @pl.when(here == 0)
        def _():
            for part in (3, 2, 1):
                to_up(unit, part, own_part(unit, part)).start()

        @pl.when(here == last)
        def _():
            for part in (0, 1, 2):
                to_down(unit, part, own_part(unit, part)).start()

    def second(unit):
        @pl.when(here == 1)
        def _():
            pass_up(unit, 3)
            pass_up(unit, 2)

        @pl.when(here == 2)
        def _():
            pass_down(unit, 0)
            pass_down(unit, 1)

    def third(unit):
        @pl.when(here == 2)
        def _():
            pass_up(unit, 3)

        @pl.when(here == 1)
        def _():
            pass_down(unit, 0)

    def finish(unit):
        slot = slot_of(unit)
        acc[...] = own[own_slot(unit), :, pl.ds(part_start(here), PART)].astype(f32)

        @pl.when(here > 0)
        def _():
            to_up(unit, here, up.at[slot, here]).wait_recv()
            acc[...] += up[slot, here].astype(f32)

        @pl.when(here < last)
        def _():
            to_down(unit, here, down.at[slot, here]).wait_recv()
            acc[...] += down[slot, here].astype(f32)

        fin[lax.rem(unit, 2)] = acc[1 - row].astype(bf16)
        swap(unit).start()
        out[slot, here, row] = acc[row].astype(bf16)

    def spread(unit):
        slot = slot_of(unit)
        for part in range(4):

            @pl.when(part > here)
            def _():
                to_up(unit, part, up.at[slot, part]).wait_send()

            @pl.when(part < here)
            def _():
                to_down(unit, part, down.at[slot, part]).wait_send()

        swap(unit).wait()

        @pl.when(here < last)
        def _():
            out_up(unit, here).start()

        @pl.when(here > 0)
        def _():
            out_down(unit, here).start()

    def relay(unit, hops):
        @pl.when(here >= hops)
        def _():
            out_up(unit, here - hops).wait_recv()

            @pl.when(here < last)
            def _():
                out_up(unit, here - hops).start()

        @pl.when(here + hops <= last)
        def _():
            out_down(unit, here + hops).wait_recv()

            @pl.when(here > 0)
            def _():
                out_down(unit, here + hops).start()

    def settle(unit):
        relay(unit, 3)
        for part in range(4):

            @pl.when((part <= here) & (here < last))
            def _():
                out_up(unit, part).wait_send()

            @pl.when((part >= here) & (here > 0))
            def _():
                out_down(unit, part).wait_send()

    def part_values(unit, side):
        slot = slot_of(unit)
        rows = [out[slot, part, side, 8 * (part % 2) : 8 * (part % 2) + 200].astype(f32) for part in range(4)]
        return jnp.concatenate(rows, 0)

    def done_copies(unit, target):
        layer, index = 1 - unit // UNITS, lax.rem(lax.rem(unit, UNITS), 6)
        return [
            pltpu.make_async_copy(
                done.at[side],
                target.at[layer, :, pl.ds(pl.multiple_of(side * WIDE + index * UNIT, UNIT), UNIT)],
                done_sem.at[side],
            )
            for side in range(2)
        ]

    def tail_copies():
        return [
            pltpu.make_async_copy(
                done_tail.at[layer, which], target.at[layer, :, pl.ds(2 * WIDE, 2 * THIN)], done_sem.at[2 + 2 * layer + which]
            )
            for layer in range(2)
            for which, target in enumerate((fc_out, proj_out))
        ]

    def frag(layer, which):
        return pltpu.make_async_remote_copy(
            src_ref=wide.at[layer, which, pl.ds(0, HDIM)],
            dst_ref=wide.at[layer, which, pl.ds(2 * STEP, HDIM)],
            send_sem=frag_send.at[layer, which],
            recv_sem=frag_recv.at[layer, which],
            device_id={"col": col - 1},
            device_id_type=MESH,
        )

    def wide_copies(layer):
        return [
            pltpu.make_async_copy(
                wide.at[layer, which, pl.ds(pl.multiple_of(16 * col, 16), COLS)],
                heads_out.at[layer, which],
                wide_sem.at[which],
            )
            for which in range(4)
        ]

    def hand_out(unit):
        local = lax.rem(unit, UNITS)
        layer = 1 - unit // UNITS
        whole = unit < 2 * UNITS

        @pl.when(whole & (local < 12))
        def _():
            for side in range(2):
                done[side] = part_values(unit, side).astype(bf16)

        for low, target in ((0, fc_out), (6, proj_out)):

            @pl.when(whole & (local >= low) & (local < low + 6))
            def _():
                for each in done_copies(unit, target):
                    each.start()

        @pl.when(whole & (local >= 12))
        def _():
            which, tile = (local - 12) // 2, lax.rem(local, 2)
            values = [part_values(unit, side).T.astype(bf16) for side in range(2)]

            @pl.when(tile == 0)
            def _():
                wide[layer, which, 0:UNIT] = values[0]
                wide[layer, which, STEP : STEP + UNIT] = values[1]

                @pl.when(col > 0)
                def _():
                    frag(layer, which).start()

            @pl.when(tile == 1)
            def _():
                wide[layer, which, UNIT:STEP] = values[0][: STEP - UNIT]
                wide[layer, which, STEP + UNIT : 2 * STEP] = values[1][: STEP - UNIT]

                @pl.when(col == 3)
                def _():
                    wide[layer, which, 2 * STEP :] = values[1][STEP - UNIT :]

        @pl.when(whole & (local == UNITS - 1))
        def _():
            for which in range(4):

                @pl.when(col < 3)
                def _():
                    frag(layer, which).wait_recv()

                @pl.when(col > 0)
                def _():
                    frag(layer, which).wait_send()

            for each in wide_copies(layer):
                each.start()

        @pl.when(unit == 2 * UNITS)
        def _():
            for side in range(2):
                value = part_values(unit, side).astype(bf16)
                for place_of in range(4):
                    done_tail[1 - place_of // 2, place_of % 2, :, side * THIN : (side + 1) * THIN] = value[
                        :, place_of * THIN : (place_of + 1) * THIN
                    ]
            for each in tail_copies():
                each.start()

    def hand_out_wait(unit):
        local = lax.rem(unit, UNITS)
        whole = unit < 2 * UNITS

        @pl.when(whole & (local < 12))
        def _():
            for each in done_copies(unit, fc_out):
                each.wait()

        @pl.when(whole & (local == UNITS - 1))
        def _():
            for each in wide_copies(1 - unit // UNITS):
                each.wait()

        @pl.when(unit == 2 * UNITS)
        def _():
            for each in tail_copies():
                each.wait()

    groups = (
        (0, 6, right_cols_pre, 1, 2),
        (6, 12, right_cols_act, 2, 3),
        (12, 18, right_cols_qkv, 0, 0),
        (18, 20, right_cols_att, 3, 1),
    )

    def terms(cols, lanes, width):
        columns = cols[:, :, lanes].reshape(8 * BLOCK, width)
        return dot_tn(columns, left_rows[...].reshape(8 * BLOCK, D)).T.astype(bf16)

    def product(unit):
        local = lax.rem(unit, UNITS)
        slot = own_slot(unit)
        for member, (low, high, cols, rows, cols_index) in enumerate(groups):
            for layer in range(2):

                @pl.when(unit == layer * UNITS + low)
                def _():
                    load_pair(layer, rows, cols_index, cols)
                    if member < 2:
                        at = (2 * layer + member) * THIN
                        tails[:, at : at + THIN] = terms(cols, slice(WIDE, WIDE + THIN), THIN)

            @pl.when((unit < 2 * UNITS) & (local >= low) & (local < high))
            def _():
                lanes = pl.ds(pl.multiple_of((local - low) * UNIT, UNIT), UNIT)
                own[slot] = terms(cols, lanes, UNIT).reshape(2, D // 2, UNIT)

        @pl.when(unit == 2 * UNITS)
        def _():
            own[slot] = tails[...].reshape(2, D // 2, UNIT)

    stages = [
        start, second, third, finish, spread,
        lambda unit: relay(unit, 1), lambda unit: relay(unit, 2), settle, hand_out, hand_out_wait,
    ]

    def tick(step, carry):
        for age in (0,) + tuple(reversed(range(1, len(stages)))):
            unit = step - 1 - age

            @pl.when((unit >= 0) & (unit < total))
            def _():
                stages[age](unit)

        @pl.when(step < total)
        def _():
            product(step)

        for hop in range(5):

            @pl.when(step == hop + 1)
            def _():
                small_step(hop)

        return carry

    lax.fori_loop(0, total + len(stages), tick, 0)


def gradient_sums(layers, small):
    flat = [array for layer in layers for array in layer]
    columns = [VMEM(array.shape, bf16) for array in layers[0][4:]]
    slots = SLOTS_DEEP
    parts = DMA((slots, 4))
    return pl.pallas_call(
        sum_gradients,
        in_specs=[pl.BlockSpec(memory_space=pl.ANY)] * len(flat) + [pl.BlockSpec(memory_space=VMEM)],
        out_specs=[pl.BlockSpec(memory_space=pl.ANY)] * 3 + [pl.BlockSpec(memory_space=VMEM)],
        out_shape=[
            jax.ShapeDtypeStruct((2, D // 2, 2 * WIDE + 2 * THIN), bf16),
            jax.ShapeDtypeStruct((2, D // 2, 2 * WIDE + 2 * THIN), bf16),
            jax.ShapeDtypeStruct((2, 4, COLS, D // 2), bf16),
            jax.ShapeDtypeStruct(small.shape, f32),
        ],
        scratch_shapes=[VMEM((4, 2, BLOCK, D), bf16)]
        + columns
        + [
            VMEM((OWN_DEEP, 2, D // 2, UNIT), bf16),
            VMEM((slots, 4, 2, PART, UNIT), bf16),
            VMEM((slots, 4, 2, PART, UNIT), bf16),
            VMEM((2, PART, UNIT), f32),
            VMEM((2, PART, UNIT), bf16),
            DMA((2,)),
            VMEM((D, UNIT), bf16),
            VMEM((slots, 4, 2, PART, UNIT), bf16),
            VMEM((2, D // 2, UNIT), bf16),
            VMEM((2, 2, D // 2, 2 * THIN), bf16),
            DMA((6,)),
            VMEM((2, 4, 2 * STEP + HDIM, D // 2), bf16),
            DMA((4,)),
            DMA((2, 4)),
            DMA((2, 4)),
        ]
        + [parts] * 4
        + [DMA((slots,))] * 2
        + [parts] * 4
        + [VMEM((3,) + small.shape, f32)] * 2
        + [VMEM((4,) + small.shape, f32)]
        + [DMA((3,))] * 2
        + [DMA((4,))] * 2,
        compiler_params=pltpu.CompilerParams(
            collective_id=6, has_side_effects=True, vmem_limit_bytes=60 << 20
        ),
        cost_estimate=pl.CostEstimate(flops=400 * 1000000000, bytes_accessed=0, transcendentals=0),
        name="sum_gradients",
    )(*flat, small)


def per_device_plane(
    tokens, cotangent, norm_gain, norm_bias, w_qkv, b_qv, w_out, out_bias, w_fc, b_fc, w_proj
):
    layers = w_qkv.shape[0]
    half_d = tokens.shape[0]
    ff = w_fc.shape[2] // 2
    row, col = lax.axis_index("row"), lax.axis_index("col")
    device = 2 * col + row

    vectors = jnp.stack([norm_gain, norm_bias, out_bias])
    vectors = partner_halves(vectors, vectors, 3)
    gains, shifts, out_shifts = vectors[0], vectors[1], vectors[2]
    fc_bias = ff_part(b_fc, row)
    qv_bias = lax.dynamic_slice_in_dim(head_window(b_qv, 2), STEP * row, WIN, 2)
    qkv_bias = jnp.concatenate([qv_bias[:, 0], jnp.zeros_like(qv_bias[:, 0]), qv_bias[:, 1]], 1)
    kept = (jnp.arange(WIN) < STEP) | (device == 7)

    def own_rows(columns):
        width = columns.shape[1] // 2
        own = lax.dynamic_slice_in_dim(columns, row * width, width, 1)
        given = lax.dynamic_slice_in_dim(columns, (1 - row) * width, width, 1)
        return partner_halves(own, given, 0).T

    def own_columns(rows):
        columns = rows.T
        own = lax.dynamic_slice_in_dim(columns, row * half_d, half_d, 0)
        given = lax.dynamic_slice_in_dim(columns, (1 - row) * half_d, half_d, 0)
        return partner_halves(own, given, 1)

    def halves(columns):
        width = columns.shape[1] // 2
        return tuple(lax.dynamic_slice_in_dim(columns, side * width, width, 1) for side in (row, 1 - row))

    stream = own_rows(tokens)
    parts = [
        (
            head_parts(w_qkv[layer].transpose(1, 2, 0).astype(bf16)),
            head_parts(w_out[layer].T[None].astype(bf16)),
            ff_parts(w_fc[layer].astype(bf16)),
            ff_parts(w_proj[layer].astype(bf16)),
        )
        for layer in range(layers)
    ]
    qkv_came, out_came, fc_came = (partner_swap(part[1]) for part in parts[0][:3])

    full_shape = ((4, 2, BLOCK, D), bf16)
    rows_shape = ((BLOCK, D), f32)
    group = lambda width, kind: ((4, 2 * BLOCK, width), kind)
    halved = lambda width: ((half_d, width), bf16)
    turned = lambda width: ((width, half_d), bf16)
    matrix = lambda width: VMEM((2, half_d, width), bf16)
    head_matrix = lambda width: VMEM((2, width, half_d), bf16)
    micros = lambda count: count * 1000000000
    saved, weights = [], []
    for layer in range(layers):
        qkv_part, out_part, fc_part, proj_part = parts[layer]
        last = layer == layers - 1
        given = (out_part, fc_part) if last else (parts[layer + 1][0], proj_part)
        shapes = [turned(WIN) if last else turned(3 * WIN), halved(ff)]
        all_one, heads, att, first_came, second_came = call(
            functools.partial(attention_forward), 7 if last else 1, "vvvhhvhh", "vvvhh",
            [full_shape, group(3 * WIN, bf16), group(WIN, bf16)] + shapes,
            [head_matrix(3 * WIN), VMEM(*group(3 * WIN, bf16)), VMEM(*group(WIN, bf16)), DMA((2,))]
            + GATHER_SCRATCH + 2 * SEQ_SCRATCH + swap_scratch(2, half_d // PIECE),
            micros(60),
            stream, gains[layer, :1], shifts[layer, :1], qkv_part[0], qkv_came, qkv_bias[layer][None],
            given[0][1], given[1][1],
        )
        if last:
            out_came, fc_came = first_came, second_came
            carried, more = (halves(cotangent)[1],), [((half_d, BLOCK), f32)]
        else:
            next_came, proj_came = first_came, second_came
            carried, more = (parts[layer + 1][3][1],), [halved(ff)]
        res, all_two, pre, act, result, moved = call(
            functools.partial(mlp_forward, last), 3 if last else 2, "vvhhvvvhhvvhhh", "vvvvvh",
            [rows_shape, full_shape, group(ff, f32), group(ff, bf16), rows_shape] + more,
            [head_matrix(WIN), matrix(ff), matrix(ff), DMA((3, 2))] + GATHER_SCRATCH
            + (swap_scratch(1, half_d // PIECE) if last else spread_scratch(1)) + 2 * SCATTER_SCRATCH,
            micros(70),
            att, stream, out_part[0], out_came, out_shifts[layer, :1], gains[layer, 1:], shifts[layer, 1:],
            fc_part[0], fc_came, fc_bias[layer][None], out_shifts[layer, 1:], proj_part[0], proj_came, *carried,
        )
        saved.append((stream, all_one, heads, att, res, all_two, pre, act))
        weights.append(
            ((qkv_part[0], qkv_came), (out_part[0], out_came), (fc_part[0], fc_came), (proj_part[0], proj_came))
        )
        stream = result
        if not last:
            qkv_came, proj_came = next_came, moved
    own_grad = halves(cotangent)[0]
    grad = jnp.concatenate(
        [jnp.where(row == 0, own_grad, moved), jnp.where(row == 0, moved, own_grad)], 0
    ).T
    vector_grads = [None] * layers
    grad_terms = []
    for layer in reversed(range(layers)):
        qkv_pair, out_pair, fc_pair, proj_pair = weights[layer]
        before, all_one, heads, att, res, all_two, pre, act = saved[layer]
        all_grad, grad_pre, all_res, grad_res, grad_att, sums = call(
            mlp_backward, 4, "vvvhhhhhhh", "vvvvvv",
            [full_shape, group(ff, bf16), full_shape, rows_shape, group(WIN, bf16), ((8, D), f32)],
            [head_matrix(WIN), matrix(ff), matrix(ff), VMEM(*group(ff, f32)), DMA((4, 2))] + 2 * GATHER_SCRATCH + SCATTER_SCRATCH,
            micros(65),
            grad, res, gains[layer, 1:], pre, *fc_pair, *proj_pair, *out_pair,
        )
        grad_qkv, grad, more_sums = call(
            attention_backward, 5, "vvvvvhh", "vvv",
            [group(3 * WIN, bf16), rows_shape, ((8, D), f32)],
            [head_matrix(3 * WIN), VMEM(*group(WIN, bf16)), VMEM(*group(WIN, f32)), VMEM(*group(WIN, f32)), VMEM(*group(3 * WIN, bf16)), DMA((2,))]
            + 2 * SEQ_SCRATCH + SCATTER_SCRATCH,
            micros(80),
            heads, grad_att, grad_res, before, gains[layer, :1], *qkv_pair,
        )
        rows = lambda values: values.reshape(8 * BLOCK, -1)
        grad_terms.append((all_one, all_two, all_grad, all_res, grad_qkv, att, grad_pre, act))
        vector_grads[layer] = (
            jnp.stack([more_sums[0], sums[1], more_sums[1], sums[2], sums[3], sums[0]]),
            jnp.sum(rows(grad_qkv).astype(f32), 0).reshape(3, WIN),
            jnp.sum(rows(grad_pre).astype(f32), 0),
        )
    slots = jnp.stack([v[1] for v in vector_grads])[:, 0::2]
    slots = jnp.where(kept, slots, jnp.zeros_like(slots))
    spread = jnp.zeros((layers, 2, D + HDIM), f32)
    spread = lax.dynamic_update_slice_in_dim(spread, slots, STEP * device, 2)[..., :D]
    hidden = jnp.zeros((layers, 8 * ff), f32)
    hidden = lax.dynamic_update_slice_in_dim(
        hidden, jnp.stack([v[2] for v in vector_grads]), ff * device, 1
    )
    small = jnp.concatenate(
        [jnp.stack([v[0] for v in vector_grads]), spread, hidden.reshape(layers, -1, D)], 1
    )
    fc_grads, proj_grads, head_grads, small = gradient_sums(grad_terms, small.reshape(-1, D))
    small = small.reshape(layers, -1, D)
    wide = lax.dynamic_slice_in_dim(small[:, :6], row * half_d, half_d, 2)
    qv_total = lax.dynamic_slice_in_dim(small[:, 6:8], col * 400, 400, 2)
    fc_total = lax.dynamic_slice_in_dim(small[:, 8:].reshape(layers, -1), col * 2 * ff, 2 * ff, 1).reshape(layers, 2, ff)
    fc_total = jnp.concatenate(
        [fc_total[:, :, :WIDE].reshape(layers, -1), fc_total[:, :, WIDE:].reshape(layers, -1)], 1
    )
    head_grads = head_grads.astype(f32)
    return (
        own_columns(stream),
        own_columns(grad),
        wide[:, 0:2],
        wide[:, 2:4],
        head_grads[:, :3].transpose(0, 3, 1, 2),
        qv_total,
        head_grads[:, 3].transpose(0, 2, 1),
        wide[:, 4:6],
        fc_grads.astype(f32),
        fc_total,
        proj_grads.astype(f32),
    )


def solution(mesh):
    in_specs = (
        P("row", ("seq", "col")),
        P("row", ("seq", "col")),
        P(None, None, "row"),
        P(None, None, "row"),
        P(None, "row", None, "col"),
        P(None, None, "col"),
        P(None, "row", "col"),
        P(None, None, "row"),
        P(None, "row", "col"),
        P(None, "col"),
        P(None, "row", "col"),
    )
    out_specs = (
        P("row", ("seq", "col")),
        P("row", ("seq", "col")),
        P(None, None, "row"),
        P(None, None, "row"),
        P(None, "row", None, "col"),
        P(None, None, "col"),
        P(None, "row", "col"),
        P(None, None, "row"),
        P(None, "row", "col"),
        P(None, "col"),
        P(None, "row", "col"),
    )
    fits = (mesh.shape["seq"], mesh.shape["row"], mesh.shape["col"]) == (4, 2, 4)
    return jax.shard_map(
        per_device_plane if fits else per_device_any, mesh=mesh, in_specs=in_specs, out_specs=out_specs, check_vma=False
    )
```

```python
import functools
import math
import types

import jax
import jax.numpy as jnp
from jax import lax
from jax.experimental import pallas as pl
from jax.experimental.pallas import tpu as pltpu
from jax.sharding import PartitionSpec as P

HEADS = 25
HDIM = 64
D = 1600
SPAN = 256
SLOTS = 4
PLANE = ("col", "row")

norm_eps = 1e-05
bf16 = jnp.bfloat16
f32 = jnp.float32


def dot_nn(left, right):
    return lax.dot_general(left, right, (((1,), (0,)), ((), ())), preferred_element_type=f32)


def dot_nt(left, right):
    return lax.dot_general(left, right, (((1,), (1,)), ((), ())), preferred_element_type=f32)


def dot_tn(left, right):
    return lax.dot_general(left, right, (((0,), (0,)), ((), ())), preferred_element_type=f32)


def swap_rows(values, split, concat):
    return lax.all_to_all(values, "row", split_axis=split, concat_axis=concat, tiled=True)


def plane_gather(values):
    return lax.all_gather(values, PLANE, axis=0, tiled=True)


def plane_sum(partial):
    return lax.psum_scatter(partial.astype(bf16), PLANE, scatter_dimension=0, tiled=True).astype(f32)


def partner_swap(values):
    count = lax.axis_size("row")
    return lax.ppermute(values, "row", [(low, low ^ 1) for low in range(count)])


def rows_to_heads(values):
    rows, parts, width = values.shape
    slots = lax.axis_size("seq") * 2 * SLOTS * HDIM
    values = jnp.pad(values, ((0, 0), (0, 0), (0, slots - width)))
    values = lax.all_to_all(values, "seq", split_axis=2, concat_axis=0, tiled=True)
    side = lax.axis_index("row") % 2
    half = SLOTS * HDIM
    own = lax.dynamic_slice_in_dim(values, side * half, half, 2)
    other = partner_swap(lax.dynamic_slice_in_dim(values, (1 - side) * half, half, 2))
    low = jnp.where(side == 0, own, other).reshape(-1, 1, rows, parts, half)
    high = jnp.where(side == 0, other, own).reshape(-1, 1, rows, parts, half)
    return jnp.concatenate([low, high], 1).reshape(-1, parts, half)


def heads_to_rows(values):
    positions, parts, half = values.shape
    count = lax.axis_size("seq")
    rows = positions // (2 * count)
    values = values.reshape(count, 2, rows, parts, half)
    side = lax.axis_index("row") % 2
    own = jnp.where(side == 0, values[:, 0], values[:, 1]).reshape(count * rows, parts, half)
    given = jnp.where(side == 0, values[:, 1], values[:, 0]).reshape(count * rows, parts, half)
    other = partner_swap(given)
    both = jnp.concatenate(
        [jnp.where(side == 0, own, other), jnp.where(side == 0, other, own)], 2
    )
    both = lax.all_to_all(both, "seq", split_axis=0, concat_axis=2, tiled=True)
    return both[:, :, :D]


def cols_to_rows(values):
    return lax.all_to_all(values, PLANE, split_axis=0, concat_axis=2, tiled=True)


def rows_to_cols(values):
    return lax.all_to_all(values, PLANE, split_axis=2, concat_axis=0, tiled=True)


def sum_weights(grad, own_shape):
    rows, cols = lax.axis_size("row"), lax.axis_size("seq")
    width = grad.shape[-1]
    split = grad.astype(bf16).reshape(rows, cols, -1, width)
    split = lax.psum_scatter(split, "seq", scatter_dimension=1, tiled=True)[:, 0]
    split = lax.all_to_all(split, "row", split_axis=0, concat_axis=0, tiled=True)
    return lax.all_gather(split, "seq", axis=0, tiled=False)


def masked_scores(query, keys, block):
    scores = dot_nt(query, keys)
    rows, width = scores.shape
    row_at = lax.broadcasted_iota(jnp.int32, (rows, width), 0) + block * rows
    col_at = lax.broadcasted_iota(jnp.int32, (rows, width), 1)
    return jnp.where(col_at <= row_at, scores, -1e30)


def softmax_rows(scores):
    weights = jnp.exp(scores - jnp.max(scores, 1, keepdims=True))
    return weights * (1.0 / jnp.sum(weights, 1, keepdims=True))


def attend_kernel(q_ref, k_ref, v_ref, out_ref):
    blocks = q_ref.shape[0] // SPAN
    for block in range(blocks):
        rows = slice(block * SPAN, (block + 1) * SPAN)
        seen = slice(0, (block + 1) * SPAN)
        parts = []
        for head in range(2):
            cols = slice(head * HDIM, (head + 1) * HDIM)
            query = q_ref[rows, cols] * bf16(HDIM**-0.5)
            weights = softmax_rows(masked_scores(query, k_ref[seen, cols], block))
            parts.append(dot_nn(weights.astype(bf16), v_ref[seen, cols]))
        out_ref[rows, :] = jnp.concatenate(parts, 1).astype(bf16)


def attend_back_kernel(q_ref, k_ref, v_ref, da_ref, dq_ref, dk_ref, dv_ref, dk_sum, dv_sum):
    blocks = q_ref.shape[0] // SPAN
    dk_sum[...] = jnp.zeros_like(dk_sum)
    dv_sum[...] = jnp.zeros_like(dv_sum)
    for block in range(blocks):
        rows = slice(block * SPAN, (block + 1) * SPAN)
        seen = slice(0, (block + 1) * SPAN)
        dq_parts, dk_parts, dv_parts = [], [], []
        for head in range(2):
            cols = slice(head * HDIM, (head + 1) * HDIM)
            query = q_ref[rows, cols] * bf16(HDIM**-0.5)
            keys, grad = k_ref[seen, cols], da_ref[rows, cols]
            weights = softmax_rows(masked_scores(query, keys, block))
            grad_weights = dot_nt(grad, v_ref[seen, cols])
            along = jnp.sum(grad_weights * weights, 1, keepdims=True)
            grad_scores = (weights * (grad_weights - along)).astype(bf16)
            dq_parts.append(dot_nn(grad_scores, keys) * HDIM**-0.5)
            dk_parts.append(dot_tn(grad_scores, query))
            dv_parts.append(dot_tn(weights.astype(bf16), grad))
        dq_ref[rows, :] = jnp.concatenate(dq_parts, 1).astype(bf16)
        dk_sum[seen, :] += jnp.concatenate(dk_parts, 1)
        dv_sum[seen, :] += jnp.concatenate(dv_parts, 1)
    dk_ref[...] = dk_sum[...].astype(bf16)
    dv_ref[...] = dv_sum[...].astype(bf16)


def attend(qkv):
    positions = qkv.shape[0]
    pairs = SLOTS // 2
    flat = qkv.reshape(positions, 3 * SLOTS * HDIM)
    spec = lambda part: pl.BlockSpec((positions, 2 * HDIM), lambda i: (0, part * pairs + i))
    return pl.pallas_call(
        attend_kernel,
        grid=(pairs,),
        in_specs=[spec(0), spec(1), spec(2)],
        out_specs=spec(0),
        out_shape=jax.ShapeDtypeStruct((positions, SLOTS * HDIM), bf16),
        compiler_params=pltpu.CompilerParams(vmem_limit_bytes=48 << 20),
        name="attend",
    )(flat, flat, flat)


def attend_back(qkv, grad):
    positions = qkv.shape[0]
    pairs = SLOTS // 2
    flat = qkv.reshape(positions, 3 * SLOTS * HDIM)
    spec = lambda part: pl.BlockSpec((positions, 2 * HDIM), lambda i: (0, part * pairs + i))
    shape = jax.ShapeDtypeStruct((positions, SLOTS * HDIM), bf16)
    grads = pl.pallas_call(
        attend_back_kernel,
        grid=(pairs,),
        in_specs=[spec(0), spec(1), spec(2), spec(0)],
        out_specs=[spec(0)] * 3,
        out_shape=[shape] * 3,
        scratch_shapes=[pltpu.VMEM((positions, 2 * HDIM), f32)] * 2,
        compiler_params=pltpu.CompilerParams(vmem_limit_bytes=48 << 20),
        name="attend_back",
    )(flat, flat, flat, grad)
    return jnp.stack(grads, 1)


def norm_forward(stream, gain, shift):
    mean_value = jnp.mean(stream, 1, keepdims=True)
    centred = stream - mean_value
    inverse = lax.rsqrt(jnp.mean(centred * centred, 1, keepdims=True) + norm_eps)
    normal_part = centred * inverse
    return ((normal_part * gain + shift).astype(bf16), normal_part, inverse)


def norm_backward(grad_out, normal_part, inverse, gain):
    scaled = grad_out * gain
    grad_in = inverse * (
        scaled
        - jnp.mean(scaled, 1, keepdims=True)
        - normal_part * jnp.mean(scaled * normal_part, 1, keepdims=True)
    )
    return (grad_in, jnp.sum(grad_out * normal_part, 0), jnp.sum(grad_out, 0))


def activation(values):
    return jax.nn.gelu(values, approximate=True)


def activation_grad(values, grad_values):
    unused_value, pullback = jax.vjp(activation, values)
    return pullback(grad_values)[0]


def per_device_any(
    tokens, cotangent, norm_gain, norm_bias, w_qkv, b_qv, w_out, out_bias, w_fc, b_fc, w_proj
):
    layers = w_qkv.shape[0]
    row_width = tokens.shape[0]
    col_width = w_out.shape[2]
    ff_width = w_fc.shape[2]
    n_rows, row = lax.axis_size("row"), lax.axis_index("row")
    own_cols, own_ff = col_width // n_rows, ff_width // n_rows

    vectors = jnp.stack([norm_gain, norm_bias, out_bias])
    vectors = lax.all_gather(vectors, "row", axis=3, tiled=True)
    gains, shifts, out_shifts = vectors[0], vectors[1], vectors[2]
    qv_bias = lax.dynamic_slice_in_dim(b_qv, row * own_cols, own_cols, 2)
    fc_bias = lax.dynamic_slice_in_dim(b_fc, row * own_ff, own_ff, 1)

    stream = swap_rows(tokens, 1, 0).T
    weights = []
    for layer in range(layers):
        qkv_matrix = swap_rows(w_qkv[layer].astype(bf16), 2, 0).reshape(D, 3 * own_cols)
        out_matrix = lax.all_gather(w_out[layer].astype(bf16), "row", axis=0, tiled=True)
        out_matrix = lax.all_gather(out_matrix, "col", axis=1, tiled=True)
        fc_matrix = swap_rows(w_fc[layer].astype(bf16), 1, 0)
        proj_matrix = swap_rows(w_proj[layer].astype(bf16), 1, 0)
        weights.append((qkv_matrix, out_matrix, fc_matrix, proj_matrix))
    saved = []
    for layer in range(layers):
        qkv_matrix, out_matrix, fc_matrix, proj_matrix = weights[layer]
        normed, normal_one, inverse_one = norm_forward(stream, gains[layer, 0], shifts[layer, 0])
        all_one = plane_gather(normed)
        bias = jnp.concatenate(
            [qv_bias[layer, 0], jnp.zeros_like(qv_bias[layer, 0]), qv_bias[layer, 1]]
        )
        qkv_cols = (dot_nn(all_one, qkv_matrix) + bias).astype(bf16)
        qkv = rows_to_heads(cols_to_rows(qkv_cols.reshape(-1, 3, own_cols)))
        attended = heads_to_rows(attend(qkv)[:, None])
        att_cols = rows_to_cols(attended)[:, 0]
        attended = attended[:, 0]
        residual = stream + (dot_nt(attended, out_matrix) + out_shifts[layer, 0])
        normed, normal_two, inverse_two = norm_forward(residual, gains[layer, 1], shifts[layer, 1])
        all_two = plane_gather(normed)
        pre_act = dot_nn(all_two, fc_matrix) + fc_bias[layer]
        act = activation(pre_act).astype(bf16)
        stream = residual + (plane_sum(dot_nt(act, proj_matrix)) + out_shifts[layer, 1])
        saved.append(
            (all_one, normal_one, inverse_one, qkv, att_cols, all_two, normal_two, inverse_two, pre_act, act)
        )
    grad_stream = swap_rows(cotangent, 1, 0).T
    grads = [None] * layers
    vector_grads = [None] * layers
    for layer in reversed(range(layers)):
        qkv_matrix, out_matrix, fc_matrix, proj_matrix = weights[layer]
        all_one, normal_one, inverse_one, qkv, att_cols, all_two, normal_two, inverse_two, pre_act, act = saved[layer]
        grad_low = grad_stream.astype(bf16)
        proj_shift = jnp.sum(grad_low.astype(f32), 0)
        all_grad = plane_gather(grad_low)
        proj_grad = sum_weights(dot_tn(all_grad, act), w_proj.shape[1:])
        grad_pre = activation_grad(pre_act, dot_nn(all_grad, proj_matrix)).astype(bf16)
        fc_grad = sum_weights(dot_tn(all_two, grad_pre), w_fc.shape[1:])
        fc_shift = jnp.sum(grad_pre.astype(f32), 0)
        grad_normed = plane_sum(dot_nt(grad_pre, fc_matrix))
        grad_in, gain_two, shift_two = norm_backward(grad_normed, normal_two, inverse_two, gains[layer, 1])
        grad_res = grad_stream + grad_in
        grad_low = grad_res.astype(bf16)
        out_shift = jnp.sum(grad_low.astype(f32), 0)
        grad_att = dot_nn(grad_low, out_matrix).astype(bf16)
        out_grad = sum_weights(dot_tn(plane_gather(grad_low), att_cols), w_out.shape[1:])
        grad_heads = rows_to_heads(grad_att[:, None])[:, 0]
        grad_rows = heads_to_rows(attend_back(qkv, grad_heads))
        grad_cols = rows_to_cols(grad_rows).reshape(-1, 3 * own_cols)
        qkv_grad = sum_weights(dot_tn(all_one, grad_cols), w_qkv.shape[1:])
        bias_sums = jnp.sum(grad_cols.astype(f32), 0).reshape(3, own_cols)
        grad_normed = plane_sum(dot_nt(grad_cols, qkv_matrix))
        grad_in, gain_one, shift_one = norm_backward(grad_normed, normal_one, inverse_one, gains[layer, 0])
        grad_stream = grad_res + grad_in
        grads[layer] = (qkv_grad, out_grad, fc_grad, proj_grad)
        vector_grads[layer] = (
            jnp.stack([jnp.stack([gain_one, gain_two]), jnp.stack([shift_one, shift_two]), jnp.stack([out_shift, proj_shift])]),
            jnp.stack([bias_sums[0], bias_sums[2]]),
            fc_shift,
        )
    wide = lax.psum(jnp.stack([v[0] for v in vector_grads]), ("seq", "col", "row"))
    wide = lax.dynamic_slice_in_dim(wide, row * row_width, row_width, 3)
    slim = jnp.concatenate(
        [jnp.concatenate([v[1].reshape(2, own_cols), v[2].reshape(ff_width // col_width, own_cols)]) for v in vector_grads]
    ).reshape(layers, -1, own_cols)
    slim_qv = lax.psum(jnp.stack([v[1] for v in vector_grads]), "seq")
    slim_fc = lax.psum(jnp.stack([v[2] for v in vector_grads]), "seq")
    qv_total = lax.all_gather(slim_qv, "row", axis=2, tiled=True)
    fc_total = lax.all_gather(slim_fc, "row", axis=1, tiled=True)

    def as_grid(member, shape):
        done = []
        for layer in range(layers):
            blocks = grads[layer][member]
            n_seq, parts = blocks.shape[:2]
            if len(shape) == 3:
                blocks = blocks.reshape(n_seq, parts, -1, 3, own_cols).transpose(0, 2, 3, 1, 4)
            else:
                blocks = blocks.transpose(0, 2, 1, 3)
            done.append(blocks.reshape(shape).astype(f32))
        return jnp.stack(done)

    return (
        swap_rows(stream.T, 0, 1),
        swap_rows(grad_stream.T, 0, 1),
        wide[:, 0],
        wide[:, 1],
        as_grid(0, w_qkv.shape[1:]),
        qv_total,
        as_grid(1, w_out.shape[1:]),
        wide[:, 2],
        as_grid(2, w_fc.shape[1:]),
        fc_total,
        as_grid(3, w_proj.shape[1:]),
    )


MESH = pl.DeviceIdType.MESH
DMA = pltpu.SemaphoreType.DMA
BLOCK = 128
WIN = SLOTS * HDIM
VMEM = pltpu.VMEM
STEP = 3 * HDIM


def place():
    col, row = lax.axis_index("col"), lax.axis_index("row")
    flip = col + 1 - 2 * lax.rem(col, 2)
    far = lax.rem(col + 2, 4)
    cross = lax.rem(flip + 2, 4)
    return col, flip, far, cross, row, 1 - row


def greet(along_seq):
    col, flip, far, cross, row, other = place()
    barrier = pltpu.get_barrier_semaphore()
    partners = [{"col": flip}, {"row": other}, {"col": far}]
    if along_seq:
        here = lax.axis_index("seq")
        partners += [{"seq": lax.rem(here + step, 4)} for step in (1, 2, 3)]
    for partner in partners:
        pl.semaphore_signal(barrier, inc=1, device_id=partner, device_id_type=MESH)
    pl.semaphore_wait(barrier, len(partners))


def remote(src, dst, send, recv, index, device):
    return pltpu.make_async_remote_copy(
        src_ref=src,
        dst_ref=dst,
        send_sem=send.at[index],
        recv_sem=recv.at[index],
        device_id=device,
        device_id_type=MESH,
    )


GATHER_SCRATCH = [DMA((10,)), DMA((10,))]


class Gather:
    def __init__(self, full, send, recv):
        col, flip, far, cross, row, other = place()
        half = BLOCK // 2
        low, high = pl.ds(0, half), pl.ds(half, half)
        core, along_x, along_y = {"col": flip}, {"row": other}, {"col": far}

        def copy(index, ref, device):
            return remote(ref, ref, send, recv, index, device)

        self.copies = [
            copy(0, full.at[col, row], core),
            copy(1, full.at[col, row, low], along_x),
            copy(2, full.at[col, row, high], along_y),
            copy(3, full.at[col, row, high], along_x),
            copy(4, full.at[col, row, low], along_y),
            copy(5, full.at[col, other, low], along_y),
            copy(6, full.at[far, row, high], along_x),
            copy(7, full.at[col, other], core),
            copy(8, full.at[far, row], core),
            copy(9, full.at[far, other], core),
        ]

    def begin(self):
        for index in (1, 2, 0, 3, 4):
            self.copies[index].start()

    def relay(self):
        for arrived, started in ((1, 5), (2, 6), (3, 7), (4, 8)):
            self.copies[arrived].wait_recv()
            self.copies[started].start()

    def corner(self):
        for arrived in (5, 6):
            self.copies[arrived].wait_recv()
        self.copies[9].start()
        for arrived in (0, 7):
            self.copies[arrived].wait_recv()

    def close(self):
        for arrived in (8, 9):
            self.copies[arrived].wait_recv()
        for each in self.copies:
            each.wait_send()


def gather(full, send, recv, body):
    col, flip, far, cross, row, other = place()
    steps = Gather(full, send, recv)
    steps.begin()
    steps.relay()
    body(col)
    steps.corner()
    body(flip)
    body(far)
    steps.close()
    body(cross)


SCATTER_SCRATCH = [
    VMEM((2, 2, BLOCK, D), bf16),
    VMEM((2, 2, BLOCK, D), bf16),
    VMEM((2, 2, BLOCK, D), bf16),
    VMEM((2, BLOCK, D), f32),
    VMEM((3, BLOCK // 2, D), bf16),
    VMEM((3, BLOCK // 2, D), bf16),
    VMEM((2, BLOCK // 2, D), bf16),
    DMA((8,)),
    DMA((8,)),
]


class Scatter:
    def __init__(self, given, taken, part, own, from_x, from_y, turn, send, recv):
        col, flip, far, cross, row, other = place()
        half = BLOCK // 2
        low, high = pl.ds(0, half), pl.ds(half, half)
        core, along_x, along_y = {"col": flip}, {"row": other}, {"col": far}
        self.given, self.taken, self.part, self.own = given, taken, part, own
        self.from_x, self.from_y, self.turned = from_x, from_y, turn
        self.low, self.high = low, high

        def copy(index, src, dst, device):
            return remote(src, dst, send, recv, index, device)

        self.sib_own = copy(0, given.at[1], taken.at[1], core)
        self.sib_far = copy(1, given.at[0], taken.at[0], core)
        self.x_far = copy(2, part.at[0, other, low], from_x.at[1], along_x)
        self.y_far = copy(3, part.at[0, other, high], from_y.at[1], along_y)
        self.y_own = copy(4, part.at[0, row, high], from_y.at[0], along_y)
        self.x_own = copy(5, part.at[1, other, low], from_x.at[0], along_x)
        self.y_turn = copy(6, turn.at[0], from_y.at[2], along_y)
        self.x_turn = copy(7, turn.at[1], from_x.at[2], along_x)

    def first(self, compute):
        col, flip, far, cross, row, other = place()
        shape = (2, BLOCK, D)
        self.given[1] = compute(flip).reshape(shape).astype(bf16)
        self.sib_own.start()
        self.given[0] = compute(cross).reshape(shape).astype(bf16)
        self.sib_far.start()

    def second(self, compute):
        col, flip, far, cross, row, other = place()
        value = compute(far).reshape(2, BLOCK, D)
        self.sib_far.wait_recv()
        self.part[0] = (value + self.taken[0].astype(f32)).astype(bf16)
        for each in (self.x_far, self.y_far, self.y_own):
            each.start()

    def third(self, compute):
        col, flip, far, cross, row, other = place()
        value = compute(col).reshape(2, BLOCK, D)
        self.sib_own.wait_recv()
        self.own[...] = value + self.taken[1].astype(f32)
        self.part[1] = self.own[...].astype(bf16)
        self.x_own.start()

    def turn(self):
        col, flip, far, cross, row, other = place()
        self.x_far.wait_recv()
        self.turned[0] = (self.part[0, row, self.low].astype(f32) + self.from_x[1].astype(f32)).astype(bf16)
        self.y_turn.start()
        self.y_far.wait_recv()
        self.turned[1] = (self.own[other, self.high] + self.from_y[1].astype(f32)).astype(bf16)
        self.x_turn.start()

    def total(self):
        row = lax.axis_index("row")
        for each in (self.x_own, self.y_own, self.y_turn, self.x_turn):
            each.wait_recv()
        total = jnp.concatenate(
            [
                self.own[row, self.low] + self.from_x[0].astype(f32) + self.from_y[2].astype(f32),
                self.own[row, self.high] + self.from_y[0].astype(f32) + self.from_x[2].astype(f32),
            ],
            0,
        )
        for each in (
            self.sib_own, self.sib_far, self.x_far, self.y_far, self.y_own, self.x_own, self.y_turn, self.x_turn
        ):
            each.wait_send()
        return total


def scatter(compute, *refs):
    steps = Scatter(*refs)
    steps.first(compute)
    steps.second(compute)
    steps.third(compute)
    steps.turn()
    return steps.total()


SEQ_SCRATCH = [DMA((4,)), DMA((4,))]


def seq_copy(src, dst, send, recv, group):
    here = lax.axis_index("seq")
    return pltpu.make_async_remote_copy(
        src_ref=src.at[group],
        dst_ref=dst.at[here],
        send_sem=send.at[group],
        recv_sem=recv.at[here],
        device_id={"seq": group},
        device_id_type=MESH,
    )


def seq_send(src, dst, send, recv, group):
    here = lax.axis_index("seq")

    @pl.when(group != here)
    def _():
        seq_copy(src, dst, send, recv, group).start()

    @pl.when(group == here)
    def _():
        dst[here] = src[here]


def seq_wait(src, dst, send, recv, group):
    @pl.when(group != lax.axis_index("seq"))
    def _():
        pltpu.make_async_remote_copy(
            src_ref=src.at[group],
            dst_ref=dst.at[group],
            send_sem=send.at[group],
            recv_sem=recv.at[group],
            device_id={"seq": group},
            device_id_type=MESH,
        ).wait_recv()


def seq_sent(src, dst, send, recv):
    for group in range(4):

        @pl.when(group != lax.axis_index("seq"))
        def _():
            seq_copy(src, dst, send, recv, group).wait_send()


class Matrix:
    def __init__(self, own, came, target, sems):
        row = lax.axis_index("row")
        self.target = target
        self.copies = [
            pltpu.make_async_copy(own, target.at[row], sems.at[0]),
            pltpu.make_async_copy(came, target.at[1 - row], sems.at[1]),
        ]

    def start(self):
        for each in self.copies:
            each.start()

    def wait(self):
        for each in self.copies:
            each.wait()

    def rows(self):
        return self.target[...].reshape(D, -1)

    def halves(self):
        return self.target[0], self.target[1]


def by_features(values, halves):
    half = D // 2
    return dot_nt(values[:, :half], halves[0]) + dot_nt(values[:, half:], halves[1])


def to_features(values, halves):
    return jnp.concatenate([dot_nn(values, halves[0]), dot_nn(values, halves[1])], 1)


PIECE = 160


def swap_scratch(arrays, pieces):
    return [DMA((arrays * pieces,)), DMA((arrays * pieces,))]


class Swaps:
    def __init__(self, pairs, send, recv):
        self.pieces, self.begun = [], 0
        for given, out in pairs:
            height = given.shape[0]
            for low in range(0, height, PIECE):
                rows = pl.ds(low, min(PIECE, height - low))
                self.pieces.append(
                    remote(given.at[rows], out.at[rows], send, recv, len(self.pieces), {"row": 1 - lax.axis_index("row")})
                )

    def start(self, count):
        for each in self.pieces[self.begun : self.begun + count]:
            each.start()
        self.begun = min(self.begun + count, len(self.pieces))

    def finish(self):
        self.start(len(self.pieces))
        for each in self.pieces:
            each.wait()


QUARTER = 192


def spread_scratch(arrays):
    return [DMA((2, arrays))] * 2 + [DMA((arrays, 4))] * 2


class Spread:
    def __init__(self, pairs, x_send, x_recv, z_send, z_recv):
        row, here = lax.axis_index("row"), lax.axis_index("seq")
        quarter = pl.ds(pl.multiple_of(here * QUARTER, 16), QUARTER)
        self.swaps, self.sends, self.waits = [], [], []
        for index, (given, out) in enumerate(pairs):
            rest = given.shape[0] - 4 * QUARTER
            ranges = (quarter, pl.ds(4 * QUARTER, rest)) if rest else (quarter,)
            for kind, rows in enumerate(ranges):
                self.swaps.append(
                    remote(given.at[rows], out.at[rows], x_send.at[kind], x_recv.at[kind], index, {"row": 1 - row})
                )
            came = out.at[quarter]
            for step in (1, 2, 3):
                to = lax.rem(here + step, 4)
                self.sends.append(
                    pltpu.make_async_remote_copy(
                        src_ref=came, dst_ref=came, send_sem=z_send.at[index, to],
                        recv_sem=z_recv.at[index, here], device_id={"seq": to}, device_id_type=MESH,
                    )
                )
                theirs = out.at[pl.ds(pl.multiple_of(to * QUARTER, 16), QUARTER)]
                self.waits.append(
                    pltpu.make_async_remote_copy(
                        src_ref=theirs, dst_ref=theirs, send_sem=z_send.at[index, to],
                        recv_sem=z_recv.at[index, to], device_id={"seq": to}, device_id_type=MESH,
                    )
                )

    def start(self):
        for each in self.swaps:
            each.start()

    def forward(self):
        for each in self.swaps:
            each.wait_recv()
        for each in self.sends:
            each.start()

    def finish(self):
        for each in self.waits:
            each.wait_recv()
        for each in self.sends + self.swaps:
            each.wait_send()


def norm_rows(stream):
    mean_value = jnp.mean(stream, 1, keepdims=True)
    centred = stream - mean_value
    inverse = lax.rsqrt(jnp.mean(centred * centred, 1, keepdims=True) + norm_eps)
    return centred * inverse, inverse


def attention_forward(last, *refs):
    count = 2 if last else 1
    stream, gain, shift, w_own, w_came, bias = refs[:6]
    given, refs = refs[6 : 6 + count], refs[6 + count :]
    full, heads, att = refs[:3]
    came, refs = refs[3 : 3 + count], refs[3 + count :]
    w, qkv, sent, w_sem, g_send, g_recv, q_send, q_recv, a_send, a_recv, *swap_sems = refs
    moves = Swaps(tuple(zip(given, came))[::-1], *swap_sems)
    col, flip, far, cross, row, other = place()
    weights = Matrix(w_own, w_came, w, w_sem)
    weights.start()
    greet(True)
    normal_part, unused = norm_rows(stream[...])
    full[col, row] = (normal_part * gain[...] + shift[...]).astype(bf16)
    seen = []

    def project(group):
        if not seen:
            weights.wait()
        seen.append(0)
        rows = full[group].reshape(2 * BLOCK, D)
        qkv[group] = (by_features(rows, weights.halves()) + bias[...]).astype(bf16)
        seq_send(qkv, heads, q_send, q_recv, group)

    gather(full, g_send, g_recv, project)
    moves.start(2)
    for block in range(4):
        seq_wait(qkv, heads, q_send, q_recv, block)
        keys_seen = (block + 1) * SPAN
        for pair in range(SLOTS // 2):
            parts = []
            for head in range(2):
                low = (2 * pair + head) * HDIM
                query = heads[block, :, low : low + HDIM] * bf16(HDIM**-0.5)
                keys = heads[: block + 1, :, WIN + low : WIN + low + HDIM].reshape(keys_seen, HDIM)
                values = heads[: block + 1, :, 2 * WIN + low : 2 * WIN + low + HDIM].reshape(keys_seen, HDIM)
                p = softmax_rows(masked_scores(query, keys, block)).astype(bf16)
                parts.append(dot_nn(p, values))
            sent[block, :, 2 * pair * HDIM : 2 * (pair + 1) * HDIM] = jnp.concatenate(parts, 1).astype(bf16)
            moves.start(1)
        seq_send(sent, att, a_send, a_recv, block)
    for block in range(4):
        seq_wait(sent, att, a_send, a_recv, block)
    seq_sent(qkv, heads, q_send, q_recv)
    seq_sent(sent, att, a_send, a_recv)
    moves.finish()


def gelu_terms(values):
    k = math.sqrt(2 / math.pi)
    squares = values * values
    t = jnp.tanh(values * (k + (k * 0.044715) * squares))
    return t, squares


def gelu_slope(values):
    t, squares = gelu_terms(values)
    k = math.sqrt(2 / math.pi)
    return 0.5 * (1 + t) + 0.5 * values * (1 - t * t) * (k + (3 * k * 0.044715) * squares)


def masked_out(matrix):
    col, flip, far, cross, row, other = place()
    kept = jnp.where(2 * col + row == 7, WIN, STEP)
    height = lax.broadcasted_iota(jnp.int32, (WIN, 1), 0)
    return [jnp.where(height < kept, half, jnp.zeros_like(half)) for half in matrix.halves()]


def mlp_forward(last, *refs):
    (att, stream, out_own, out_came, out_shift, gain, shift, fc_own, fc_came, fc_bias, proj_shift,
     proj_own, proj_came) = refs[:13]
    count = 1 if last else 2
    given, refs = refs[13 : 13 + count], refs[13 + count :]
    res, full, pre, act, result = refs[:5]
    came, refs = refs[5 : 5 + count], refs[5 + count :]
    w_out, fc, proj, w_sem, g_send, g_recv, *scratch = refs
    if last:
        moves = Swaps(tuple(zip(given, came)), *scratch[:2])
        scratch = scratch[2:]
    else:
        spread = Spread(tuple(zip(given, came)), *scratch[:4])
        scratch = scratch[4:]
    col, flip, far, cross, row, other = place()
    out_matrix = Matrix(out_own, out_came, w_out, w_sem.at[0])
    fc_matrix = Matrix(fc_own, fc_came, fc, w_sem.at[1])
    proj_matrix = Matrix(proj_own, proj_came, proj, w_sem.at[2])
    out_matrix.start()
    fc_matrix.start()
    proj_matrix.start()
    greet(not last)
    out_matrix.wait()
    count = len(SCATTER_SCRATCH)
    w_out_rows = masked_out(out_matrix)
    if not last:
        spread.start()

    asked = []

    def out_terms(group):
        asked.append(group)
        if last:
            moves.start(1)
        elif len(asked) == 4:
            spread.forward()
        return to_features(att[group], w_out_rows)

    total = scatter(out_terms, *scratch[:count])
    res[...] = stream[...] + (total + out_shift[...])
    normal_part, unused = norm_rows(res[...])
    full[col, row] = (normal_part * gain[...] + shift[...]).astype(bf16)
    seen = []

    def widen(group):
        if not seen:
            fc_matrix.wait()
        seen.append(0)
        u = dot_nn(full[group].reshape(2 * BLOCK, D), fc_matrix.rows()) + fc_bias[...]
        pre[group] = u
        t, unused = gelu_terms(u)
        act[group] = (0.5 * u * (1 + t)).astype(bf16)

    gather(full, g_send, g_recv, widen)
    if last:
        moves.finish()
    proj_matrix.wait()
    total = scatter(lambda group: dot_nt(act[group], proj_matrix.rows()), *scratch[count:])
    result[...] = res[...] + (total + proj_shift[...])
    if not last:
        spread.finish()


def norm_back_rows(grad_out, normal_part, inverse, gain):
    scaled = grad_out * gain
    return inverse * (
        scaled
        - jnp.mean(scaled, 1, keepdims=True)
        - normal_part * jnp.mean(scaled * normal_part, 1, keepdims=True)
    )


def mlp_backward(
    grad, res, gain, pre_hbm, fc_own, fc_came, proj_own, proj_came, out_own, out_came,
    full, grad_pre, full_res, grad_res, grad_att, sums,
    w_out, fc, proj, pre, w_sem, g_send, g_recv, h_send, h_recv, *scratch,
):
    col, flip, far, cross, row, other = place()
    out_matrix = Matrix(out_own, out_came, w_out, w_sem.at[0])
    fc_matrix = Matrix(fc_own, fc_came, fc, w_sem.at[1])
    proj_matrix = Matrix(proj_own, proj_came, proj, w_sem.at[2])
    pre_copy = pltpu.make_async_copy(pre_hbm, pre, w_sem.at[3, 0])
    proj_matrix.start()
    pre_copy.start()
    fc_matrix.start()
    out_matrix.start()
    greet(False)
    low = grad[...].astype(bf16)
    full[col, row] = low
    sums[0:1, :] = jnp.sum(low.astype(f32), 0, keepdims=True)
    seen = []

    def widen(group):
        if not seen:
            proj_matrix.wait()
            pre_copy.wait()
        seen.append(0)
        grad_act = dot_nn(full[group].reshape(2 * BLOCK, D), proj_matrix.rows())
        u = pre[group]
        grad_pre[group] = (grad_act * gelu_slope(u)).astype(bf16)

    gather(full, g_send, g_recv, widen)
    fc_matrix.wait()
    total = scatter(lambda group: dot_nt(grad_pre[group], fc_matrix.rows()), *scratch)
    normal_part, inverse = norm_rows(res[...])
    sums[1:2, :] = jnp.sum(total * normal_part, 0, keepdims=True)
    sums[2:3, :] = jnp.sum(total, 0, keepdims=True)
    grad_res[...] = grad[...] + norm_back_rows(total, normal_part, inverse, gain[...])
    low = grad_res[...].astype(bf16)
    full_res[col, row] = low
    sums[3:4, :] = jnp.sum(low.astype(f32), 0, keepdims=True)
    sums[4:8, :] = jnp.zeros((4, D), f32)

    out_matrix.wait()
    w_out_rows = masked_out(out_matrix)

    def out_back(group):
        grad_att[group] = by_features(full_res[group].reshape(2 * BLOCK, D), w_out_rows).astype(bf16)

    gather(full_res, h_send, h_recv, out_back)


def attend_back_block(block, heads, da, dk, dv, sent):
    keys_seen = (block + 1) * SPAN
    for pair in range(SLOTS // 2):
        dq_parts, dk_parts, dv_parts = [], [], []
        for head in range(2):
            low = (2 * pair + head) * HDIM
            query = heads[block, :, low : low + HDIM] * bf16(HDIM**-0.5)
            keys = heads[: block + 1, :, WIN + low : WIN + low + HDIM].reshape(keys_seen, HDIM)
            values = heads[: block + 1, :, 2 * WIN + low : 2 * WIN + low + HDIM].reshape(keys_seen, HDIM)
            grad = da[block, :, low : low + HDIM]
            p = softmax_rows(masked_scores(query, keys, block))
            dp = dot_nt(grad, values)
            ds = (p * (dp - jnp.sum(dp * p, 1, keepdims=True))).astype(bf16)
            dq_parts.append(dot_nn(ds, keys) * HDIM**-0.5)
            dk_parts.append(dot_tn(ds, query))
            dv_parts.append(dot_tn(p.astype(bf16), grad))
        cols = slice(2 * pair * HDIM, 2 * (pair + 1) * HDIM)
        new_dk = jnp.concatenate(dk_parts, 1).reshape(block + 1, SPAN, 2 * HDIM)
        new_dv = jnp.concatenate(dv_parts, 1).reshape(block + 1, SPAN, 2 * HDIM)
        if block < 3:
            new_dk = new_dk + dk[: block + 1, :, cols]
            new_dv = new_dv + dv[: block + 1, :, cols]
        dk[: block + 1, :, cols] = new_dk
        dv[: block + 1, :, cols] = new_dv
        sent[block, :, cols] = jnp.concatenate(dq_parts, 1).astype(bf16)
    sent[block, :, WIN : 2 * WIN] = dk[block].astype(bf16)
    sent[block, :, 2 * WIN :] = dv[block].astype(bf16)


def call(kernel, ident, places, out_places, outs, scratch, cost, *operands):
    spaces = {"v": VMEM, "h": pl.ANY}
    return pl.pallas_call(
        kernel,
        in_specs=[pl.BlockSpec(memory_space=spaces[each]) for each in places],
        out_specs=[pl.BlockSpec(memory_space=spaces[each]) for each in out_places],
        out_shape=[jax.ShapeDtypeStruct(shape, kind) for shape, kind in outs],
        scratch_shapes=scratch,
        compiler_params=pltpu.CompilerParams(
            collective_id=ident, has_side_effects=True, vmem_limit_bytes=60 << 20
        ),
        cost_estimate=pl.CostEstimate(flops=cost, bytes_accessed=0, transcendentals=0),
        name=getattr(kernel, "func", kernel).__name__,
    )(*operands)


def partner_halves(own, given, axis):
    row = lax.axis_index("row")
    other = partner_swap(given)
    return jnp.concatenate(
        [jnp.where(row == 0, own, other), jnp.where(row == 0, other, own)], axis
    )


def ff_part(block, side):
    axis = block.ndim - 1
    full, wide = block.shape[axis] // 2, WIDE
    thin = full - wide
    return jnp.concatenate(
        [
            lax.dynamic_slice_in_dim(block, side * wide, wide, axis),
            lax.dynamic_slice_in_dim(block, 2 * wide + side * thin, thin, axis),
        ],
        axis,
    )


def split_rows(*refs):
    own_side = lax.axis_index("row") == 0
    for index in range(2):
        for layer in range(2):
            rows = refs[index][layer].astype(bf16)
            sides = [
                jnp.concatenate(
                    [rows[:, side * WIDE : (side + 1) * WIDE], rows[:, 2 * WIDE + side * THIN : 2 * WIDE + (side + 1) * THIN]], 1
                )
                for side in range(2)
            ]
            at = 2 + 4 * index + 2 * layer
            refs[at][...] = jnp.where(own_side, sides[0], sides[1])
            refs[at + 1][...] = jnp.where(own_side, sides[1], sides[0])


def ff_parts(first, second):
    layers, rows, width = first.shape
    part = jax.ShapeDtypeStruct((rows, width // 2), bf16)
    parts = pl.pallas_call(
        split_rows,
        grid=(rows // PIECE,),
        in_specs=[pl.BlockSpec((layers, PIECE, width), lambda i: (0, i, 0))] * 2,
        out_specs=[pl.BlockSpec((PIECE, width // 2), lambda i: (i, 0))] * 8,
        out_shape=[part] * 8,
        compiler_params=pltpu.CompilerParams(vmem_limit_bytes=48 << 20),
        cost_estimate=pl.CostEstimate(flops=0, bytes_accessed=31 << 20, transcendentals=0),
        name="split_rows",
    )(first, second)
    return [[tuple(parts[4 * index + 2 * layer : 4 * index + 2 * layer + 2]) for layer in range(2)] for index in range(2)]


def head_window(block, axis):
    col = lax.axis_index("col")
    edge = 3 * 16
    last = lax.slice_in_dim(block, block.shape[axis] - edge, block.shape[axis], axis=axis)
    left = lax.ppermute(last, "col", [(0, 1), (1, 2), (2, 3)])
    wide = jnp.concatenate([left, block, jnp.zeros_like(last)], axis)
    return lax.dynamic_slice_in_dim(wide, edge - 16 * col, 2 * STEP + HDIM, axis)


def head_parts(block):
    row = lax.axis_index("row")
    wide = head_window(block, 1)
    parts = [lax.dynamic_slice_in_dim(wide, side * STEP, WIN, 1) for side in (row, 1 - row)]
    return tuple(part.reshape(-1, part.shape[2]) for part in parts)


UNIT = 128
WIDE = 6 * UNIT
UNITS = 20
THIN = 32
COLS = 400
SLOTS_DEEP = 6
OWN_DEEP = 5
PART = 208
LAST = 3


def rem(value, count):
    return value % count if isinstance(value, int) else lax.rem(value, count)


def aligned(value, unit):
    return value if isinstance(value, int) else pl.multiple_of(value, unit)


def when(condition):
    if isinstance(condition, bool):
        return lambda act: act() if condition else None
    return pl.when(condition)


def part_start(part):
    return aligned(200 * part - 8 * rem(part, 2), 16)


IN_NAMES = (
    "n1_b n2_b eh_b er_b dpre_b act_b att_b heads_b datt_b dres_b stream_b gain1_b qkv_own_b qkv_came_b sums_b "
    "n1_a n2_a act_a att_a heads_a res_a stream_a gain1_a gain2_a qkv_own_a qkv_came_a "
    "pre_a fc_own_a fc_came_a proj_own_a proj_came_a out_own_a out_came_a"
).split()
IN_VMEM = ("datt_b", "gain1_b", "sums_b", "gain1_a", "gain2_a")
OUT_NAMES = "fc_out proj_out heads_out small_out result eh_a er_a".split()
SMALL_ROWS = 32


def backward_scratch():
    slots, parts = SLOTS_DEEP, DMA((SLOTS_DEEP, 4))
    wide_rows = VMEM((4, 2, BLOCK, D), bf16)
    group = lambda width, kind: VMEM((4, 2 * BLOCK, width), kind)
    ff = WIDE + THIN
    flow = VMEM((slots, 4, 2, PART, UNIT), bf16)
    return dict(
        left_rows=wide_rows, cols=group(ff, bf16), own=VMEM((OWN_DEEP, 2, D // 2, UNIT), bf16), up=flow, down=flow,
        acc=VMEM((2, PART, UNIT), f32), fin=VMEM((2, PART, UNIT), bf16), load=DMA((2,)), tails=VMEM((D, UNIT), bf16),
        out=flow, done=VMEM((2, D // 2, UNIT), bf16), done_tail=VMEM((2, 2, D // 2, 2 * THIN), bf16), done_sem=DMA((6,)),
        turned=VMEM((2, UNIT, D // 2), bf16), turned_sem=DMA((2, 8)), frag_send=DMA((3,)), frag_recv=DMA((8, 3)),
        up_send=parts, up_recv=parts, down_send=parts, down_recv=parts, swap_send=DMA((slots,)), swap_recv=DMA((slots,)),
        out_up_send=parts, out_up_recv=parts, out_down_send=parts, out_down_recv=parts,
        stage=VMEM((3, SMALL_ROWS, D), f32), inbox=VMEM((3, SMALL_ROWS, D), f32), line=VMEM((4, SMALL_ROWS, D), f32),
        s_send=DMA((3,)), s_recv=DMA((3,)), l_send=DMA((4,)), l_recv=DMA((4,)),
        full=wide_rows, big=VMEM((2, D // 2, ff), bf16), big_sem=DMA((2,)), w_out=VMEM((2, WIN, D // 2), bf16),
        out_sem=DMA((2,)), pre=group(ff, f32), pre_sem=DMA((1,)), dpre=group(ff, bf16), heads=group(3 * WIN, bf16),
        heads_sem=DMA((1,)), da=VMEM((2, 4, 2 * BLOCK, WIN), bf16), datt=group(WIN, bf16), dk=group(WIN, f32),
        dv=group(WIN, f32), sent=group(3 * WIN, bf16), dqkv=VMEM((2, 4, 2 * BLOCK, 3 * WIN), bf16),
        grad=VMEM((BLOCK, D), f32), dres=VMEM((BLOCK, D), f32), rows=VMEM((BLOCK, D), f32), rows_sem=DMA((1,)),
        dres_sem=DMA((1,)), store_sem=DMA((1,)), g_send=DMA((10,)), g_recv=DMA((10,)),
        a_send=DMA((4,)), a_recv=DMA((4,)), q_send=DMA((4,)), q_recv=DMA((4,)),
        **{"scatter_%d" % index: each for index, each in enumerate(SCATTER_SCRATCH)},
    )


def backward(names, *refs):
    r = types.SimpleNamespace(**dict(zip(names, refs)))
    own, up, down, acc, fin, out, done, done_tail = r.own, r.up, r.down, r.acc, r.fin, r.out, r.done, r.done_tail
    up_send, up_recv, down_send, down_recv = r.up_send, r.up_recv, r.down_send, r.down_recv
    out_up_send, out_up_recv, out_down_send, out_down_recv = r.out_up_send, r.out_up_recv, r.out_down_send, r.out_down_recv
    swap_send, swap_recv, done_sem, left_rows = r.swap_send, r.swap_recv, r.done_sem, r.left_rows
    stage, inbox, line = r.stage, r.inbox, r.line
    s_send, s_recv, l_send, l_recv = r.s_send, r.s_recv, r.l_send, r.l_recv
    small_out, fc_out, proj_out, heads_out, turned = r.small_out, r.fc_out, r.proj_out, r.heads_out, r.turned
    here = lax.axis_index("seq")
    total = 2 * UNITS + 1
    last = LAST
    col, flip, far, cross, row, other = place()
    device = 2 * col + row
    near = [{"col": flip}, {"row": other}, {"col": far}]
    barrier = pltpu.get_barrier_semaphore()
    partners = [{"row": other}] + [{axis: lax.rem(index + step, 4)} for axis, index in (("col", col), ("seq", here)) for step in (1, 2, 3)]
    for partner in partners:
        pl.semaphore_signal(barrier, inc=1, device_id=partner, device_id_type=MESH)
    pl.semaphore_wait(barrier, len(partners))

    def small_copy(hop):
        return remote(stage.at[hop], inbox.at[hop], s_send, s_recv, hop, near[hop])

    def line_copy(step):
        to = lax.rem(here + step, 4)
        return pltpu.make_async_remote_copy(
            src_ref=line.at[here], dst_ref=line.at[here], send_sem=l_send.at[to],
            recv_sem=l_recv.at[here], device_id={"seq": to}, device_id_type=MESH,
        )

    def line_wait(step):
        start = lax.rem(here + step, 4)
        pltpu.make_async_remote_copy(
            src_ref=line.at[start], dst_ref=line.at[start], send_sem=l_send.at[start],
            recv_sem=l_recv.at[start], device_id={"seq": start}, device_id_type=MESH,
        ).wait_recv()

    def small_step(hop):
        if hop == 0:
            small_copy(0).start()
        elif hop < 3:
            small_copy(hop - 1).wait()
            stage[hop] = stage[hop - 1] + inbox[hop - 1]
            small_copy(hop).start()
        elif hop == 3:
            small_copy(2).wait()
            line[here] = stage[2] + inbox[2]
            for step in (1, 2, 3):
                line_copy(step).start()
        else:
            for step in (1, 2, 3):
                line_wait(step)
                line_copy(step).wait_send()
            small_out[...] = (line[0] + line[1]) + (line[2] + line[3])

    def slot_of(unit):
        return rem(unit, SLOTS_DEEP)

    def own_slot(unit):
        return rem(unit, OWN_DEEP)

    def own_part(unit, part):
        return own.at[own_slot(unit), :, pl.ds(part_start(part), PART)]

    def to_up(unit, part, src):
        slot = slot_of(unit)
        return pltpu.make_async_remote_copy(
            src_ref=src, dst_ref=up.at[slot, part], send_sem=up_send.at[slot, part],
            recv_sem=up_recv.at[slot, part], device_id={"seq": here + 1}, device_id_type=MESH,
        )

    def to_down(unit, part, src):
        slot = slot_of(unit)
        return pltpu.make_async_remote_copy(
            src_ref=src, dst_ref=down.at[slot, part], send_sem=down_send.at[slot, part],
            recv_sem=down_recv.at[slot, part], device_id={"seq": here - 1}, device_id_type=MESH,
        )

    def pass_up(unit, part):
        slot = slot_of(unit)
        to_up(unit, part, up.at[slot, part]).wait_recv()
        add = own[own_slot(unit), :, pl.ds(part_start(part), PART)].astype(f32)
        up[slot, part] = (up[slot, part].astype(f32) + add).astype(bf16)
        to_up(unit, part, up.at[slot, part]).start()

    def pass_down(unit, part):
        slot = slot_of(unit)
        to_down(unit, part, down.at[slot, part]).wait_recv()
        add = own[own_slot(unit), :, pl.ds(part_start(part), PART)].astype(f32)
        down[slot, part] = (down[slot, part].astype(f32) + add).astype(bf16)
        to_down(unit, part, down.at[slot, part]).start()

    def swap(unit):
        slot = slot_of(unit)
        return remote(
            fin.at[rem(unit, 2)], out.at[slot, here, row], swap_send, swap_recv, slot, {"row": 1 - row}
        )

    def out_up(unit, part):
        slot = slot_of(unit)
        ref = out.at[slot, part]
        return pltpu.make_async_remote_copy(
            src_ref=ref, dst_ref=ref, send_sem=out_up_send.at[slot, part],
            recv_sem=out_up_recv.at[slot, part], device_id={"seq": here + 1}, device_id_type=MESH,
        )

    def out_down(unit, part):
        slot = slot_of(unit)
        ref = out.at[slot, part]
        return pltpu.make_async_remote_copy(
            src_ref=ref, dst_ref=ref, send_sem=out_down_send.at[slot, part],
            recv_sem=out_down_recv.at[slot, part], device_id={"seq": here - 1}, device_id_type=MESH,
        )

    def start(unit):
        @when(here == 0)
        def _():
            for part in (3, 2, 1):
                to_up(unit, part, own_part(unit, part)).start()

        @when(here == last)
        def _():
            for part in (0, 1, 2):
                to_down(unit, part, own_part(unit, part)).start()

    def second(unit):
        @when(here == 1)
        def _():
            pass_up(unit, 3)
            pass_up(unit, 2)

        @when(here == 2)
        def _():
            pass_down(unit, 0)
            pass_down(unit, 1)

    def third(unit):
        @when(here == 2)
        def _():
            pass_up(unit, 3)

        @when(here == 1)
        def _():
            pass_down(unit, 0)

    def finish(unit):
        slot = slot_of(unit)
        acc[...] = own[own_slot(unit), :, pl.ds(part_start(here), PART)].astype(f32)

        @when(here > 0)
        def _():
            to_up(unit, here, up.at[slot, here]).wait_recv()
            acc[...] += up[slot, here].astype(f32)

        @when(here < last)
        def _():
            to_down(unit, here, down.at[slot, here]).wait_recv()
            acc[...] += down[slot, here].astype(f32)

        fin[rem(unit, 2)] = acc[1 - row].astype(bf16)
        swap(unit).start()
        out[slot, here, row] = acc[row].astype(bf16)

    def spread(unit):
        slot = slot_of(unit)
        for part in range(4):

            @when(part > here)
            def _():
                to_up(unit, part, up.at[slot, part]).wait_send()

            @when(part < here)
            def _():
                to_down(unit, part, down.at[slot, part]).wait_send()

        swap(unit).wait()

        @when(here < last)
        def _():
            out_up(unit, here).start()

        @when(here > 0)
        def _():
            out_down(unit, here).start()

    def relay(unit, hops):
        @when(here >= hops)
        def _():
            out_up(unit, here - hops).wait_recv()

            @when(here < last)
            def _():
                out_up(unit, here - hops).start()

        @when(here + hops <= last)
        def _():
            out_down(unit, here + hops).wait_recv()

            @when(here > 0)
            def _():
                out_down(unit, here + hops).start()

    def settle(unit):
        relay(unit, 3)
        for part in range(4):

            @when((part <= here) & (here < last))
            def _():
                out_up(unit, part).wait_send()

            @when((part >= here) & (here > 0))
            def _():
                out_down(unit, part).wait_send()

    def part_values(unit, side):
        slot = slot_of(unit)
        rows = [out[slot, part, side, 8 * (part % 2) : 8 * (part % 2) + 200].astype(f32) for part in range(4)]
        return jnp.concatenate(rows, 0)

    def done_copies(unit, target):
        layer, index = 1 - unit // UNITS, rem(rem(unit, UNITS), 6)
        return [
            pltpu.make_async_copy(
                done.at[side],
                target.at[layer, :, pl.ds(aligned(side * WIDE + index * UNIT, UNIT), UNIT)],
                done_sem.at[side],
            )
            for side in range(2)
        ]

    def tail_copies():
        return [
            pltpu.make_async_copy(
                done_tail.at[layer, which], target.at[layer, :, pl.ds(2 * WIDE, 2 * THIN)], done_sem.at[2 + 2 * layer + which]
            )
            for layer in range(2)
            for which, target in enumerate((fc_out, proj_out))
        ]

    def head_place(unit):
        local = rem(unit, UNITS)
        return 1 - unit // UNITS, rem((local - 12) // 2 + 3, 4), rem(local, 2)

    def head_copies(unit, act):
        layer, which, tile = head_place(unit)
        for side in range(2):
            for piece in range(8):
                at = 2 * HDIM * tile + 16 * piece
                if side == 0:
                    kept = (at >= 16 * col) & (at < STEP)
                else:
                    kept = (at < STEP) | (col == 3)
                if side == 1 and isinstance(at, int) and at < STEP:
                    kept = True

                @when(kept)
                def _():
                    target = aligned(side * STEP + at - 16 * col, 16)
                    act(
                        pltpu.make_async_copy(
                            turned.at[side, pl.ds(16 * piece, 16)],
                            heads_out.at[layer, which, pl.ds(target, 16)],
                            r.turned_sem.at[side, piece],
                        )
                    )

    def frag(layer, which, piece):
        return pltpu.make_async_remote_copy(
            src_ref=turned.at[0, pl.ds(16 * piece, 16)],
            dst_ref=heads_out.at[layer, which, pl.ds(aligned(2 * STEP + 16 * piece - 16 * (col - 1), 16), 16)],
            send_sem=r.frag_send.at[piece],
            recv_sem=r.frag_recv.at[4 * layer + which, piece],
            device_id={"col": col - 1},
            device_id_type=MESH,
        )

    def frags(unit, act):
        layer, which, tile = head_place(unit)
        for piece in range(3):

            if isinstance(tile, int) and tile > 0:
                continue

            @when((tile == 0) & (piece < col))
            def _():
                act(frag(layer, which, piece))

    def frags_arrived():
        for layer in range(2):
            for which in range(4):
                for piece in range(3):

                    @when((piece <= col) & (col < 3))
                    def _():
                        pltpu.make_async_remote_copy(
                            src_ref=turned.at[0, pl.ds(16 * piece, 16)],
                            dst_ref=heads_out.at[layer, which, pl.ds(aligned(2 * STEP + 16 * piece - 16 * col, 16), 16)],
                            send_sem=r.frag_send.at[piece],
                            recv_sem=r.frag_recv.at[4 * layer + which, piece],
                            device_id={"col": col + 1},
                            device_id_type=MESH,
                        ).wait_recv()

    def hand_out(unit):
        local = rem(unit, UNITS)
        whole = unit < 2 * UNITS

        @when(whole & (local < 12))
        def _():
            for side in range(2):
                done[side] = part_values(unit, side).astype(bf16)

        for low, target in ((0, fc_out), (6, proj_out)):

            @when(whole & (local >= low) & (local < low + 6))
            def _():
                for each in done_copies(unit, target):
                    each.start()

        @when(whole & (local >= 12))
        def _():
            for side in range(2):
                turned[side] = part_values(unit, side).T.astype(bf16)
            head_copies(unit, lambda each: each.start())
            frags(unit, lambda each: each.start())

        @when(unit == 2 * UNITS)
        def _():
            for side in range(2):
                value = part_values(unit, side).astype(bf16)
                for place_of in range(4):
                    done_tail[1 - place_of // 2, place_of % 2, :, side * THIN : (side + 1) * THIN] = value[
                        :, place_of * THIN : (place_of + 1) * THIN
                    ]
            for each in tail_copies():
                each.start()

    def hand_out_wait(unit):
        local = rem(unit, UNITS)
        whole = unit < 2 * UNITS

        @when(whole & (local < 12))
        def _():
            for each in done_copies(unit, fc_out):
                each.wait()

        @when(whole & (local >= 12))
        def _():
            head_copies(unit, lambda each: each.wait())
            frags(unit, lambda each: each.wait_send())

        @when(unit == 2 * UNITS)
        def _():
            for each in tail_copies():
                each.wait()

    groups = (
        (0, 6, ((r.n2_b, r.cols, r.dpre_b), (r.n2_a, r.dpre, None))),
        (6, 12, ((r.eh_b, r.cols, r.act_b), (r.eh_a, r.cols, r.act_a))),
        (12, 14, ((r.er_b, r.cols, r.att_b), (r.er_a, r.cols, r.att_a))),
        (14, 20, ((r.n1_b, r.dqkv.at[0], None), (r.n1_a, r.dqkv.at[1], None))),
    )

    def load_pair(left, cols, source):
        pair = [pltpu.make_async_copy(left, left_rows, r.load.at[0])]
        if source is not None:
            target = cols if source.shape[-1] == cols.shape[-1] else cols.at[:, :, : source.shape[-1]]
            pair.append(pltpu.make_async_copy(source, target, r.load.at[1]))
        for each in pair:
            each.start()
        for each in pair:
            each.wait()

    def terms(cols, lanes, width):
        columns = cols[:, :, lanes].reshape(8 * BLOCK, width)
        return dot_tn(columns, left_rows[...].reshape(8 * BLOCK, D)).T.astype(bf16)

    def column_sums(cols, low, high):
        return jnp.sum(jnp.sum(cols[:, :, low:high].astype(f32), 0), 0, keepdims=True)

    def product(unit):
        slot = own_slot(unit)
        for member, (low, high, sides) in enumerate(groups):
            for order, (left, cols, source) in enumerate(sides):
                first = order * UNITS + low
                if not isinstance(unit, int) and first + high - low <= len(steps):
                    continue
                mine = pl.ds(12 + 8 * order + device, 1)

                @when(unit == first)
                def _():
                    load_pair(left, cols, source)
                    if member < 2:
                        at = (2 * order + member) * THIN
                        r.tails[:, at : at + THIN] = terms(cols, slice(WIDE, WIDE + THIN), THIN)
                    if member == 0:
                        stage[0, mine, 2 * WIN : 2 * WIN + WIDE + THIN] = column_sums(cols, 0, WIDE + THIN)
                    if member == 3:
                        stage[0, mine, :WIN] = column_sums(cols, 0, WIN)
                        stage[0, mine, WIN : 2 * WIN] = column_sums(cols, 2 * WIN, 3 * WIN)

                @when((unit >= first) & (unit < first + high - low))
                def _():
                    lanes = pl.ds(aligned((unit - first) * UNIT, UNIT), UNIT)
                    own[slot] = terms(cols, lanes, UNIT).reshape(2, D // 2, UNIT)

        @when(unit == 2 * UNITS)
        def _():
            own[slot] = r.tails[...].reshape(2, D // 2, UNIT)


    def one_copy(src, dst, sem):
        return pltpu.make_async_copy(src, dst, sem.at[0])

    head_rows = r.big.at[:, : 3 * WIN]
    qkv_matrix = (Matrix(r.qkv_own_b, r.qkv_came_b, head_rows, r.big_sem), Matrix(r.qkv_own_a, r.qkv_came_a, head_rows, r.big_sem))
    proj_matrix = Matrix(r.proj_own_a, r.proj_came_a, r.big, r.big_sem)
    fc_matrix = Matrix(r.fc_own_a, r.fc_came_a, r.big, r.big_sem)
    out_matrix = Matrix(r.out_own_a, r.out_came_a, r.w_out, r.out_sem)
    heads_copy = (one_copy(r.heads_b, r.heads, r.heads_sem), one_copy(r.heads_a, r.heads, r.heads_sem))
    rows_copy = [one_copy(src, r.rows, r.rows_sem) for src in (r.stream_b, r.res_a, r.stream_a)]
    dres_copy = one_copy(r.dres_b, r.dres, r.dres_sem)
    pre_copy = one_copy(r.pre_a, r.pre, r.pre_sem)
    meet = Scatter(*[getattr(r, "scatter_%d" % index) for index in range(len(SCATTER_SCRATCH))])
    spread_out = Gather(r.full, r.g_send, r.g_recv)
    attention_sends = ((r.datt_b, r.da.at[0]), (r.datt, r.da.at[1]))

    def rows_of(group):
        return r.full[group].reshape(2 * BLOCK, D)

    def begin():
        stage[0] = jnp.zeros((SMALL_ROWS, D), f32)
        for at, source in ((7, 1), (9, 2), (10, 3), (11, 0)):
            stage[0, at : at + 1] = r.sums_b[source : source + 1]
        for each in (qkv_matrix[0], out_matrix, heads_copy[0], rows_copy[0], dres_copy, pre_copy):
            each.start()
        for group in range(4):
            seq_send(*attention_sends[0], r.a_send, r.a_recv, group)

    def attention_steps(order, result, base):
        source, da = attention_sends[order]
        dqkv = r.dqkv.at[order]
        compute = lambda group: to_features(dqkv[group], qkv_matrix[order].halves())

        def queries(block):
            if block == 3:
                heads_copy[order].wait()
            seq_wait(source, da, r.a_send, r.a_recv, block)
            attend_back_block(block, r.heads, da, r.dk, r.dv, r.sent)
            seq_send(r.sent, dqkv, r.q_send, r.q_recv, block)

        def meeting():
            for block in range(4):
                seq_wait(r.sent, dqkv, r.q_send, r.q_recv, block)
            if order == 0:
                heads_copy[1].start()
            qkv_matrix[order].wait()
            meet.first(compute)

        def ending():
            grad_out = meet.total()
            rows_copy[2 * order].wait()
            if order == 0:
                dres_copy.wait()
            normal_part, inverse = norm_rows(r.rows[...])
            stage[0, base : base + 1] = jnp.sum(grad_out * normal_part, 0, keepdims=True)
            stage[0, base + 2 : base + 3] = jnp.sum(grad_out, 0, keepdims=True)
            gain = (r.gain1_b, r.gain1_a)[order]
            result[...] = r.dres[...] + norm_back_rows(grad_out, normal_part, inverse, gain[...])
            if order == 0:
                rows_copy[1].start()
            seq_sent(source, da, r.a_send, r.a_recv)
            seq_sent(r.sent, dqkv, r.q_send, r.q_recv)

        def third():
            meet.third(compute)
            if order == 0:
                proj_matrix.start()

        return [functools.partial(queries, block) for block in (3, 2, 1, 0)] + [
            meeting, lambda: meet.second(compute), third, meet.turn, ending
        ]

    def widen(group):
        grad_act = dot_nn(rows_of(group), proj_matrix.rows())
        r.dpre[group] = (grad_act * gelu_slope(r.pre[group])).astype(bf16)

    def fc_terms(group):
        return dot_nt(r.dpre[group], fc_matrix.rows())

    def mlp_start():
        low = r.grad[...].astype(bf16)
        r.full[col, row] = low
        stage[0, 5:6] = jnp.sum(low.astype(f32), 0, keepdims=True)
        spread_out.begin()

    def mlp_relay():
        spread_out.relay()
        proj_matrix.wait()
        pre_copy.wait()
        widen(col)

    def mlp_corner():
        spread_out.corner()
        widen(flip)
        widen(far)

    def mlp_close():
        spread_out.close()
        widen(cross)
        one_copy(r.full, r.eh_a, r.store_sem).start()
        fc_matrix.start()

    def mlp_meeting():
        one_copy(r.full, r.eh_a, r.store_sem).wait()
        fc_matrix.wait()
        meet.first(fc_terms)

    def mlp_third():
        meet.third(fc_terms)
        qkv_matrix[1].start()

    def mlp_ending():
        grad_out = meet.total()
        rows_copy[1].wait()
        normal_part, inverse = norm_rows(r.rows[...])
        stage[0, 1:2] = jnp.sum(grad_out * normal_part, 0, keepdims=True)
        stage[0, 3:4] = jnp.sum(grad_out, 0, keepdims=True)
        r.dres[...] = r.grad[...] + norm_back_rows(grad_out, normal_part, inverse, r.gain2_a[...])
        rows_copy[2].start()
        low = r.dres[...].astype(bf16)
        r.full[col, row] = low
        stage[0, 4:5] = jnp.sum(low.astype(f32), 0, keepdims=True)
        spread_out.begin()

    def out_back(group):
        r.datt[group] = by_features(rows_of(group), masked_out(out_matrix)).astype(bf16)
        seq_send(*attention_sends[1], r.a_send, r.a_recv, group)

    def out_relay():
        spread_out.relay()
        out_matrix.wait()
        out_back(col)

    def out_corner():
        spread_out.corner()
        out_back(flip)
        out_back(far)

    def out_close():
        spread_out.close()
        out_back(cross)
        one_copy(r.full, r.er_a, r.store_sem).start()

    def out_stored():
        one_copy(r.full, r.er_a, r.store_sem).wait()

    steps = attention_steps(0, r.grad, 6)
    steps += [mlp_start, mlp_relay, mlp_corner, mlp_close, mlp_meeting, lambda: meet.second(fc_terms), mlp_third, meet.turn]
    steps += [mlp_ending, out_relay, out_corner, out_close]
    more = attention_steps(1, r.result, 0)
    queries_first = more[0]

    def stored_and_queries():
        out_stored()
        queries_first()

    steps += [stored_and_queries] + more[1:]
    first_small = len(steps) + 4

    stages = [
        start, second, third, finish, spread,
        lambda unit: relay(unit, 1), lambda unit: relay(unit, 2), settle, hand_out, hand_out_wait,
    ]

    def tick(step, carry):
        for age in (0,) + tuple(reversed(range(1, len(stages)))):
            unit = step - 1 - age

            @when((unit >= 0) & (unit < total))
            def _():
                stages[age](unit)

        @when(step < total)
        def _():
            product(step)

        if isinstance(step, int):
            steps[step]()
            return None
        for hop in range(5):

            @when(step == first_small + hop)
            def _():
                small_step(hop)

        return carry

    begin()
    for step in range(len(steps)):
        tick(step, None)
    lax.fori_loop(len(steps), total + len(stages), tick, 0)
    frags_arrived()


def run_backward(operands, ff):
    scratch = backward_scratch()
    half = D // 2
    names = tuple(IN_NAMES) + tuple(OUT_NAMES) + tuple(scratch)
    spaces = [VMEM if name in IN_VMEM else pl.ANY for name in IN_NAMES]
    hbm, vmem = pl.BlockSpec(memory_space=pl.ANY), pl.BlockSpec(memory_space=VMEM)
    outs = pl.pallas_call(
        functools.partial(backward, names),
        in_specs=[pl.BlockSpec(memory_space=space) for space in spaces],
        out_specs=[hbm, hbm, hbm, vmem, vmem, hbm, hbm],
        out_shape=[
            jax.ShapeDtypeStruct((2, half, 2 * ff), bf16),
            jax.ShapeDtypeStruct((2, half, 2 * ff), bf16),
            jax.ShapeDtypeStruct((2, 4, COLS, half), bf16),
            jax.ShapeDtypeStruct((SMALL_ROWS, D), f32),
            jax.ShapeDtypeStruct((BLOCK, D), f32),
            jax.ShapeDtypeStruct((4, 2, BLOCK, D), bf16),
            jax.ShapeDtypeStruct((4, 2, BLOCK, D), bf16),
        ],
        scratch_shapes=list(scratch.values()),
        compiler_params=pltpu.CompilerParams(collective_id=6, has_side_effects=True, vmem_limit_bytes=63 << 20),
        cost_estimate=pl.CostEstimate(flops=500 * 1000000000, bytes_accessed=0, transcendentals=0),
        name="backward",
    )(*[operands[name] for name in IN_NAMES])
    return outs[:5]


def per_device_plane(
    tokens, cotangent, norm_gain, norm_bias, w_qkv, b_qv, w_out, out_bias, w_fc, b_fc, w_proj
):
    layers = w_qkv.shape[0]
    half_d = tokens.shape[0]
    ff = w_fc.shape[2] // 2
    row, col = lax.axis_index("row"), lax.axis_index("col")

    vectors = jnp.stack([norm_gain, norm_bias, out_bias])
    vectors = partner_halves(vectors, vectors, 3)
    gains, shifts, out_shifts = vectors[0], vectors[1], vectors[2]
    fc_bias = ff_part(b_fc, row)
    qv_bias = lax.dynamic_slice_in_dim(head_window(b_qv, 2), STEP * row, WIN, 2)
    qkv_bias = jnp.concatenate([qv_bias[:, 0], jnp.zeros_like(qv_bias[:, 0]), qv_bias[:, 1]], 1)
    def own_rows(columns):
        width = columns.shape[1] // 2
        own = lax.dynamic_slice_in_dim(columns, row * width, width, 1)
        given = lax.dynamic_slice_in_dim(columns, (1 - row) * width, width, 1)
        return partner_halves(own, given, 0).T

    def own_columns(rows):
        columns = rows.T
        own = lax.dynamic_slice_in_dim(columns, row * half_d, half_d, 0)
        given = lax.dynamic_slice_in_dim(columns, (1 - row) * half_d, half_d, 0)
        return partner_halves(own, given, 1)

    def halves(columns):
        width = columns.shape[1] // 2
        return tuple(lax.dynamic_slice_in_dim(columns, side * width, width, 1) for side in (row, 1 - row))

    stream = own_rows(tokens)
    first = head_parts(w_qkv[0].transpose(1, 2, 0).astype(bf16))
    qkv_came = partner_swap(first[1])
    w_fc, w_proj, w_out, later_qkv, unused = lax.optimization_barrier((w_fc, w_proj, w_out, w_qkv[1], first[1]))
    fc_parts, proj_parts = ff_parts(w_fc, w_proj)
    out_parts = [head_parts(w_out[layer].T[None].astype(bf16)) for layer in range(layers)]
    out_came = partner_swap(out_parts[0][1])
    quarter = half_d // 4
    fc_came = lax.dynamic_slice_in_dim(fc_parts[0][1], lax.axis_index("seq") * quarter, quarter, 0)
    fc_came = lax.all_gather(partner_swap(fc_came), "seq", axis=0, tiled=True)
    parts = [
        (first, out_parts[0], fc_parts[0], proj_parts[0]),
        (head_parts(later_qkv.transpose(1, 2, 0).astype(bf16)), out_parts[1], fc_parts[1], proj_parts[1]),
    ]

    full_shape = ((4, 2, BLOCK, D), bf16)
    rows_shape = ((BLOCK, D), f32)
    group = lambda width, kind: ((4, 2 * BLOCK, width), kind)
    halved = lambda width: ((half_d, width), bf16)
    turned = lambda width: ((width, half_d), bf16)
    matrix = lambda width: VMEM((2, half_d, width), bf16)
    head_matrix = lambda width: VMEM((2, width, half_d), bf16)
    micros = lambda count: count * 1000000000
    saved, weights = [], []
    for layer in range(layers):
        qkv_part, out_part, fc_part, proj_part = parts[layer]
        last = layer == layers - 1
        given = (out_part, fc_part) if last else (proj_part,)
        shapes = [turned(WIN), halved(ff)] if last else [halved(ff)]
        all_one, heads, att, *moved = call(
            functools.partial(attention_forward, last), 7 if last else 1, "vvvhhv" + len(given) * "h", "vvv" + len(given) * "h",
            [full_shape, group(3 * WIN, bf16), group(WIN, bf16)] + shapes,
            [head_matrix(3 * WIN), VMEM(*group(3 * WIN, bf16)), VMEM(*group(WIN, bf16)), DMA((2,))]
            + GATHER_SCRATCH + 2 * SEQ_SCRATCH + swap_scratch(len(given), half_d // PIECE),
            micros(60),
            stream, gains[layer, :1], shifts[layer, :1], qkv_part[0], qkv_came, qkv_bias[layer][None],
            *(part[1] for part in given),
        )
        if last:
            out_came, fc_came = moved
            carried, more = (halves(cotangent)[1],), [((half_d, BLOCK), f32)]
        else:
            proj_came = moved[0]
            carried, more = (parts[layer + 1][0][1], parts[layer + 1][3][1]), [turned(3 * WIN), halved(ff)]
        res, all_two, pre, act, result, *moved = call(
            functools.partial(mlp_forward, last), 3 if last else 2, "vvhhvvvhhvvhh" + len(more) * "h", "vvvvv" + len(more) * "h",
            [rows_shape, full_shape, group(ff, f32), group(ff, bf16), rows_shape] + more,
            [head_matrix(WIN), matrix(ff), matrix(ff), DMA((3, 2))] + GATHER_SCRATCH
            + (swap_scratch(1, half_d // PIECE) if last else spread_scratch(2)) + 2 * SCATTER_SCRATCH,
            micros(70),
            att, stream, out_part[0], out_came, out_shifts[layer, :1], gains[layer, 1:], shifts[layer, 1:],
            fc_part[0], fc_came, fc_bias[layer][None], out_shifts[layer, 1:], proj_part[0], proj_came, *carried,
        )
        saved.append((stream, all_one, heads, att, res, all_two, pre, act))
        weights.append(
            ((qkv_part[0], qkv_came), (out_part[0], out_came), (fc_part[0], fc_came), (proj_part[0], proj_came))
        )
        stream = result
        if not last:
            qkv_came, proj_came = moved
    own_grad = halves(cotangent)[0]
    grad = jnp.concatenate(
        [jnp.where(row == 0, own_grad, moved[0]), jnp.where(row == 0, moved[0], own_grad)], 0
    ).T
    qkv_pair, out_pair, fc_pair, proj_pair = weights[1]
    before, all_one, heads, att, res, all_two, pre, act = saved[1]
    all_grad, grad_pre, all_res, grad_res, grad_att, sums = call(
        mlp_backward, 4, "vvvhhhhhhh", "vvvvvv",
        [full_shape, group(ff, bf16), full_shape, rows_shape, group(WIN, bf16), ((8, D), f32)],
        [head_matrix(WIN), matrix(ff), matrix(ff), VMEM(*group(ff, f32)), DMA((4, 2))] + 2 * GATHER_SCRATCH + SCATTER_SCRATCH,
        micros(65),
        grad, res, gains[1, 1:], pre, *fc_pair, *proj_pair, *out_pair,
    )
    operands = dict(
        n1_b=all_one, n2_b=all_two, eh_b=all_grad, er_b=all_res, dpre_b=grad_pre, act_b=act, att_b=att, heads_b=heads,
        datt_b=grad_att, dres_b=grad_res, stream_b=before, gain1_b=gains[1, :1], qkv_own_b=qkv_pair[0],
        qkv_came_b=qkv_pair[1], sums_b=sums,
    )
    qkv_pair, out_pair, fc_pair, proj_pair = weights[0]
    before, all_one, heads, att, res, all_two, pre, act = saved[0]
    operands.update(
        n1_a=all_one, n2_a=all_two, act_a=act, att_a=att, heads_a=heads, res_a=res, stream_a=before,
        gain1_a=gains[0, :1], gain2_a=gains[0, 1:], qkv_own_a=qkv_pair[0], qkv_came_a=qkv_pair[1], pre_a=pre,
        fc_own_a=fc_pair[0], fc_came_a=fc_pair[1], proj_own_a=proj_pair[0], proj_came_a=proj_pair[1],
        out_own_a=out_pair[0], out_came_a=out_pair[1],
    )
    fc_grads, proj_grads, head_grads, small, grad = run_backward(operands, ff)
    wide = lax.dynamic_slice_in_dim(small[:12].reshape(layers, 6, D), row * half_d, half_d, 2)
    each = small[12:28].reshape(2, 8, D)[::-1]
    pairs = jnp.moveaxis(each[:, :, : 2 * WIN].reshape(layers, 8, 2, WIN), 1, 2)
    qv_total = jnp.concatenate([pairs[:, :, :7, :STEP].reshape(layers, 2, 7 * STEP), pairs[:, :, 7]], 2)
    qv_total = lax.dynamic_slice_in_dim(qv_total, col * 400, 400, 2)
    fc_total = lax.dynamic_slice_in_dim(each[:, :, 2 * WIN : 2 * WIN + ff], 2 * col, 2, 1)
    fc_total = jnp.concatenate(
        [fc_total[:, :, :WIDE].reshape(layers, -1), fc_total[:, :, WIDE:].reshape(layers, -1)], 1
    )
    head_grads = head_grads.astype(f32)
    return (
        own_columns(stream),
        own_columns(grad),
        wide[:, 0:2],
        wide[:, 2:4],
        head_grads[:, :3].transpose(0, 3, 1, 2),
        qv_total,
        head_grads[:, 3].transpose(0, 2, 1),
        wide[:, 4:6],
        fc_grads.astype(f32),
        fc_total,
        proj_grads.astype(f32),
    )


def solution(mesh):
    in_specs = (
        P("row", ("seq", "col")),
        P("row", ("seq", "col")),
        P(None, None, "row"),
        P(None, None, "row"),
        P(None, "row", None, "col"),
        P(None, None, "col"),
        P(None, "row", "col"),
        P(None, None, "row"),
        P(None, "row", "col"),
        P(None, "col"),
        P(None, "row", "col"),
    )
    out_specs = (
        P("row", ("seq", "col")),
        P("row", ("seq", "col")),
        P(None, None, "row"),
        P(None, None, "row"),
        P(None, "row", None, "col"),
        P(None, None, "col"),
        P(None, "row", "col"),
        P(None, None, "row"),
        P(None, "row", "col"),
        P(None, "col"),
        P(None, "row", "col"),
    )
    fits = (mesh.shape["seq"], mesh.shape["row"], mesh.shape["col"]) == (4, 2, 4)
    return jax.shard_map(
        per_device_plane if fits else per_device_any, mesh=mesh, in_specs=in_specs, out_specs=out_specs, check_vma=False
    )
```
